32 devices in a mesh: narrow: 4 (over y, core), wide: 8 (over z, x).
Axes of the slice: x: 2, y: 2, z: 4, core: 2. Of those that a mesh axis runs over, the one named last changes fastest.
Arguments:
- inputs: bfloat16 [256, 8, 100], P('wide'), may hold values from -6 to 6
- cotangent: bfloat16 [256, 8, 10], P('wide'), may hold values from -6 to 6
- step_mask: int32 [256, 8], P('wide'), may hold values 0 or 1
- washout: int32 [256], P('wide'), may hold values from 0 to 1
- lengths: int32 [256], P('wide'), may hold values from 4 to 8
- leak_groups: int32 [2, 4, 2048], P(None, 'narrow'), may hold values 0 or 1
- leak_two: float32 [4], P('narrow'), may hold values from 0.03 to 0.3
- w_one: bfloat16 [4, 2048, 2048], P('narrow'), may hold values from -0.125 to 0.125
- v_one: bfloat16 [4, 100, 2048], P('narrow'), may hold values from -0.625 to 0.625
- v_two: bfloat16 [4, 2048, 2048], P('narrow'), may hold values from -0.25 to 0.25
- w_two: bfloat16 [4, 2048, 2048], P('narrow'), may hold values from -0.125 to 0.125
- w_out: bfloat16 [8192, 10], P('narrow'), may hold values from -0.0625 to 0.0625
- b_out: float32 [10], replicated, may hold values from -4 to 4
Outputs:
- output: float32 [256, 8, 10], P('wide', 'narrow')
- input_grad: float32 [256, 8, 100], P('wide')
- grad_w_one: float32 [4, 2048, 2048], P('narrow', None, 'wide')
- grad_v_one: float32 [4, 100, 2048], P('narrow', None, 'wide')
- grad_v_two: float32 [4, 2048, 2048], P('narrow', None, 'wide')
- grad_w_two: float32 [4, 2048, 2048], P('narrow', None, 'wide')
- grad_w_out: float32 [8192, 10], P('narrow')
- grad_b_out: float32 [10], replicated
The draws below stay inside these ranges and needn't reach their ends.
All inputs are finite; a program needn't handle non-finite values. No bound on the sum of `step_mask` or of `leak_groups` on one device may be relied on, other than what follows from the above.
Results may differ from the reference program's by a relative error of at most 0.0055.
Values may be sent and summed in bfloat16 or wider, within the bound.
No kernel may reach another device: no remote copies, remote signals or barrier semaphores. Data moves between devices by JAX's collectives and lax.ppermute only.
A program may use at most 192 MiB of HBM per device.

```python
import math
import jax
import jax.numpy as jnp
from jax import lax

UNITS = 2048
INPUTS = 100
OUTPUTS = 10
STEPS = 8
MEMBERS = 4
SEQS = 256
FEATURES = 8192


def touch_ends(result, stream_key, least, largest):
    index_at = [jax.random.randint(jax.random.fold_in(stream_key, axis), (), 0, length) for axis, length in enumerate(result.shape)]
    widest = result.shape.index(max(result.shape))
    next_to = index_at[:widest] + [(index_at[widest] + 1) % result.shape[widest]] + index_at[widest + 1:]
    return result.at[tuple(index_at)].set(least).at[tuple(next_to)].set(largest)


def steps_of(stream_key, shape, pieces, least, top_value):
    factor_of, own = 1.0, jax.random.fold_in(stream_key, 6)
    for axis_at, parts in pieces:
        draws = jnp.exp(jax.random.uniform(jax.random.fold_in(own, axis_at), (parts,), jnp.float32, least / len(pieces), top_value / len(pieces)))
        factor_of = factor_of * jnp.repeat(draws, shape[axis_at] // parts).reshape([-1 if axis == axis_at else 1 for axis in range(len(shape))])
    return factor_of


def gaussian(own_key, extent, scale, bound, split=(), kind=jnp.bfloat16):
    array = jax.random.normal(own_key, extent, jnp.float32) * scale
    if len(split) > 0:
        array = steps_of(own_key, extent, split, -0.22, 0.18) * array
    return jnp.clip(array, min=-bound, max=bound).astype(kind)


def setup_inputs(seed: int = 0) -> dict:
    keys = jax.random.split(jax.random.key(seed), 14)
    inputs = gaussian(keys[0], (SEQS, STEPS, INPUTS), 1.0, 6.0, ((0, 8),))
    cotangent = gaussian(keys[1], (SEQS, STEPS, OUTPUTS), 1.0, 6.0, ((0, 8),))
    step_mask = touch_ends((jax.random.randint(keys[2], (SEQS, STEPS), 0, 8) < 7).astype(jnp.int32), jax.random.fold_in(keys[2], 1), 0, 1)
    washout = touch_ends(jax.random.randint(keys[3], (SEQS,), 0, STEPS // 4), jax.random.fold_in(keys[3], 1), 0, (STEPS // 4) - 1).astype(jnp.int32)
    lengths = touch_ends(jax.random.randint(keys[4], (SEQS,), STEPS // 2, STEPS + 1), jax.random.fold_in(keys[4], 1), STEPS // 2, STEPS).astype(jnp.int32)
    leak_groups = touch_ends((jax.random.randint(keys[5], (2, MEMBERS, UNITS), 0, 2) < 1).astype(jnp.int32), jax.random.fold_in(keys[5], 1), 0, 1)
    leak_two = jnp.clip(jnp.exp(math.log(0.3) - 2.3025852 * jax.random.uniform(keys[6], (MEMBERS,), jnp.float32) ** steps_of(keys[6], (MEMBERS,), ((0, 4),), -0.2, 0.2)), 0.03, 0.3)
    w_one = gaussian(keys[7], (MEMBERS, UNITS, UNITS), (UNITS * 100 // 81) ** -0.5, 0.125, ((0, 4),))
    v_one = gaussian(keys[8], (MEMBERS, INPUTS, UNITS), INPUTS ** -0.5, 0.625, ((0, 4),))
    v_two = gaussian(keys[9], (MEMBERS, UNITS, UNITS), (UNITS // 4) ** -0.5, 0.25, ((0, 4),))
    w_two = gaussian(keys[10], (MEMBERS, UNITS, UNITS), (UNITS * 100 // 81) ** -0.5, 0.125, ((0, 4),))
    w_out = gaussian(keys[11], (FEATURES, OUTPUTS), FEATURES ** -0.5, 0.0625, ((0, 4),))
    b_out = gaussian(keys[12], (OUTPUTS,), 1.0, 4.0, (), jnp.float32)
    return dict(inputs=inputs, cotangent=cotangent, step_mask=step_mask, washout=washout, lengths=lengths, leak_groups=leak_groups, leak_two=leak_two, w_one=w_one, v_one=v_one, v_two=v_two, w_two=w_two, w_out=w_out, b_out=b_out)


@jax.custom_vjp
def low(v):
    return lax.optimization_barrier(v.astype(jnp.bfloat16)).astype(jnp.float32)

@jax.custom_vjp
def lowered_backward(v):
    return v

def low_keep(v):
    return (low(v), None)

def low_pass(kept, grad):
    return (grad,)

def back_keep(v):
    return (v, None)

def back_low(kept, grad):
    return (low(grad),)
low.defvjp(low_keep, low_pass)
lowered_backward.defvjp(back_keep, back_low)
HIGH_PRECISION = lax.Precision.HIGHEST

def reference(inputs, cotangent, step_mask, washout, lengths, leak_groups, leak_two, w_one, v_one, v_two, w_two, w_out, b_out):
    rates = jnp.where(leak_groups == 0, jnp.float32(0.3), leak_two[None, :, None]).astype(jnp.float32)
    rate_one = rates[0][:, None, :]
    rate_two = rates[1][:, None, :]
    position = jnp.arange(STEPS, dtype=jnp.int32)[None, :]
    valid = ((step_mask == 1) & (position >= washout[:, None]) & (position < lengths[:, None])).astype(jnp.float32)
    members = w_one.shape[0]
    seqs = inputs.shape[0]

    def forward(source, input_weight_first, recurrent_weight_first, recurrent_weight_second, input_weight_second, head, bias):
        series = jnp.transpose(source, (1, 0, 2))

        def advance(carry, current_input):
            h_one, h_two, leaky_state_first, leaky_state_second = carry
            preactivation_first = lowered_backward(jnp.einsum('une,uex->unx', leaky_state_first, input_weight_first, precision=HIGH_PRECISION) + jnp.einsum('jx,axb->ajb', current_input, recurrent_weight_first, precision=HIGH_PRECISION))
            h_one = (1.0 - rate_one) * h_one + rate_one * jnp.tanh(preactivation_first)
            leaky_state_first = low(h_one)
            preactivation_second = lowered_backward(jnp.einsum('une,uex->unx', leaky_state_second, input_weight_second, precision=HIGH_PRECISION) + jnp.einsum('une,uex->unx', leaky_state_first, recurrent_weight_second, precision=HIGH_PRECISION))
            h_two = (1.0 - rate_two) * h_two + rate_two * jnp.tanh(preactivation_second)
            leaky_state_second = low(h_two)
            return ((h_one, h_two, leaky_state_first, leaky_state_second), leaky_state_second)
        zero_state = jnp.zeros((members, seqs, UNITS), jnp.float32)
        start = (zero_state, zero_state, zero_state, zero_state)
        final, states = lax.scan(jax.checkpoint(advance), start, series)
        feats = lowered_backward(states)
        whole = jnp.transpose(feats, (2, 0, 1, 3)).reshape(seqs, STEPS, members * UNITS)
        weights = valid[:, :, None]
        count = jnp.sum(valid)
        mean = lax.optimization_barrier(jnp.sum(weights * whole, axis=(0, 1))) / count
        square = lax.optimization_barrier(jnp.sum(weights * whole * whole, axis=(0, 1))) / count
        inv = lax.rsqrt(square - mean * mean + 1e-05)
        normed = low((whole - mean) * inv)
        return jnp.einsum('slf,fo->slo', normed, head, precision=HIGH_PRECISION) + bias
    output, pullback = jax.vjp(forward, inputs.astype(jnp.float32), w_one.astype(jnp.float32), v_one.astype(jnp.float32), v_two.astype(jnp.float32), w_two.astype(jnp.float32), w_out.astype(jnp.float32), b_out)
    grads = pullback(cotangent.astype(jnp.float32) * valid[:, :, None])
    return (output, grads[0], grads[1], grads[2], grads[3], grads[4], grads[5], grads[6])
```

```python
import functools

import jax
import jax.numpy as jnp
from jax import lax
from jax.experimental import pallas as pl
from jax.experimental.pallas import tpu as pltpu
from jax.sharding import PartitionSpec as P

F32 = jnp.float32
BF16 = jnp.bfloat16
LANES = 128
ROW0 = 96
TILE = 512
VMEM = pl.BlockSpec(memory_space=pltpu.VMEM)
ANY = pl.BlockSpec(memory_space=pl.ANY)
ROWS_T = (((0,), (0,)), ((), ()))
COLS_T = (((1,), (1,)), ((), ()))


def mm(a, b):
    return jnp.dot(a, b, preferred_element_type=F32)


def mm_rows(a, b):
    return lax.dot_general(a, b, ROWS_T, preferred_element_type=F32)


def mm_cols(a, b):
    return lax.dot_general(a, b, COLS_T, preferred_element_type=F32)


def set_of(index, sets):
    return (index ^ (index >> 1)) & (sets - 1)


def tiles(width, tile=TILE):
    return [pl.ds(n, tile) for n in range(0, width, tile)]


def own_rank(members):
    me = lax.axis_index("wide")
    return functools.reduce(
        lambda a, b: a + b, [(jnp.bitwise_xor(me, d) < me).astype(jnp.int32) for d in members[1:]]
    )


def forward_kernel(members, lanes, *refs):
    blocks = refs[: len(members)]
    wx, rates, w1h, v2h, w2h = refs[len(members) : len(members) + 5]
    lo1h, lo2h, s1h, s2h, stats, packs = refs[len(members) + 5 : len(members) + 11]
    (w1, v2, w2, lo1, lo2, s1, s2, a1, b1, a2, b2, h1, h2, ssq, wsem, osem) = refs[len(members) + 11 :]
    steps, rows, units = lo1.shape
    shard = blocks[0].shape[1]
    loads = [
        pltpu.make_async_copy(v2h, v2, wsem.at[0]),
        pltpu.make_async_copy(w1h, w1, wsem.at[1]),
        pltpu.make_async_copy(w2h, w2, wsem.at[2]),
    ]
    for load in loads:
        load.start()
    me = lax.axis_index("wide")
    for d, block in zip(members, blocks):
        rank = functools.reduce(
            lambda a, b: a + b,
            [
                (jnp.bitwise_xor(me, e) < jnp.bitwise_xor(me, d)).astype(jnp.int32)
                for e in members
                if e != d
            ],
            jnp.int32(0),
        )
        at = pl.ds(pl.multiple_of(rank * shard, shard), shard)
        for t in range(steps):
            packs[t, at, :] = block[t]
    ssq[...] = jnp.zeros_like(ssq)

    def layer_one(t, prev, new):
        for n in tiles(units):
            acc = mm(packs[t], wx[:, n])
            if prev is not None:
                acc = acc + mm(prev[...], w1[:, n])
            th = jnp.tanh(acc)
            r = rates[0:1, n]
            if prev is None:
                h = r * th
            else:
                h = h1[:, n]
                h = h + r * (th - h)
            low = h.astype(BF16)
            h1[:, n] = h
            new[:, n] = low
            lo1[t, :, n] = low
            s1[t, :, n] = (r * (1.0 - th * th)).astype(s1.dtype)

    def layer_two(t, below, prev, new):
        valid = packs[t][:, lanes - 1 : lanes].astype(F32)
        for n in tiles(units):
            acc = mm(below[...], v2[:, n])
            if prev is not None:
                acc = acc + mm(prev[...], w2[:, n])
            th = jnp.tanh(acc)
            r = rates[1:2, n]
            if prev is None:
                h = r * th
            else:
                h = h2[:, n]
                h = h + r * (th - h)
            low = h.astype(BF16)
            h2[:, n] = h
            new[:, n] = low
            lo2[t, :, n] = low
            s2[t, :, n] = (r * (1.0 - th * th)).astype(s2.dtype)
            f = low.astype(F32)
            ssq[:, n] += jnp.sum((f * f * valid).reshape(rows // 8, 8, f.shape[1]), axis=0)

    def out_copies(t):
        return [
            pltpu.make_async_copy(src.at[t], dst.at[t], osem.at[i, t])
            for i, (src, dst) in enumerate(((lo1, lo1h), (s1, s1h), (lo2, lo2h), (s2, s2h)))
        ]

    def step(t, p1, n1, p2, n2):
        layer_one(t, p1, n1)
        layer_two(t, n1, p2, n2)
        for copy in out_copies(t):
            copy.start()

    layer_one(0, None, a1)
    loads[0].wait()
    layer_two(0, a1, None, a2)
    for copy in out_copies(0):
        copy.start()
    loads[1].wait()
    loads[2].wait()

    def pair(i, carry):
        t = 1 + 2 * i
        step(t, a1, b1, a2, b2)
        step(t + 1, b1, a1, b2, a2)
        return carry

    lax.fori_loop(0, (steps - 2) // 2, pair, 0)
    step(steps - 1, a1, b1, a2, b2)
    every = packs[...].reshape(steps * rows, LANES)
    for n in tiles(units):
        both = mm_rows(every, lo2[:, :, n].reshape(steps * rows, TILE))
        stats[:, n] = both[ROW0 : ROW0 + 16]
        stats[15:16, n] = jnp.sum(ssq[:, n], axis=0, keepdims=True)
    stats[:, units : units + LANES] = mm_rows(every, every)[ROW0 : ROW0 + 16]
    for t in range(steps):
        for copy in out_copies(t):
            copy.wait()


def back_steps(steps, dh, bufs, dp_all, weight, rate_of, extra_of, slope_of, ready, done):
    units = dh.shape[1]

    def one(t, now, later):
        ready(t - 1)
        for n in tiles(units):
            r = rate_of(n)
            grad = (1.0 - r) * dh[:, n] + mm(now[...], weight[:, n])
            grad = grad + extra_of(t - 1, n)
            low = (grad * slope_of(t - 1, n)).astype(BF16)
            dh[:, n] = grad
            later[:, n] = low
            dp_all[t - 1, :, n] = low
        done(t - 1)

    def pair(i, carry):
        t = steps - 1 - 2 * i
        one(t, bufs[0], bufs[1])
        one(t - 1, bufs[1], bufs[0])
        return carry

    lax.fori_loop(0, (steps - 2) // 2, pair, 0)
    one(1, bufs[0], bufs[1])


def partial_grads(left, steps, shift, dp_all, cols, width, own, sends, own_stage, send_stage, sems, out):
    units = left.shape[2]
    rows = left.shape[1]
    half = units // 2
    count = steps - shift
    for side in range(2):
        for place, block in enumerate((cols[0], cols[1 + side])):
            at = pl.ds(pl.multiple_of(block * width, LANES), width)
            sends[:, pl.ds(place * width, width)] = dp_all[:, :, at].reshape(steps * rows, width)
        right = sends[shift * rows :, :]
        for m in range(0, half, TILE):
            at = pl.ds(side * half + m, TILE)
            l = left[:count, :, at].reshape(count * rows, TILE)
            both = mm_rows(l, right)
            own_stage[at, :] = both[:, :width]
            send_stage[at, :] = both[:, width:].astype(BF16)
    copies = [
        pltpu.make_async_copy(own_stage, own, sems.at[0]),
        pltpu.make_async_copy(send_stage.at[pl.ds(0, half)], out[0], sems.at[1]),
        pltpu.make_async_copy(send_stage.at[pl.ds(half, half)], out[1], sems.at[2]),
    ]
    for copy in copies:
        copy.start()
    return copies


def back_two_kernel(members, lanes, outputs, narrow, partners, width, *refs):
    st_own, st_other, wg, rates, packs, lo1h, lo2h, s2h, w2h = refs[:9]
    pieces, gwo, dp2h = refs[9:12]
    rest = refs[12:]
    if partners:
        own_w, w_a, w_b, own_v, v_a, v_b = rest[:6]
        rest = rest[6:]
    (lo1, lo2, s2, w2, dp2, dh, bufa, bufb, coef, lsem, wsem, osem) = rest[:12]
    if partners:
        sends, own_ws, send_ws, own_vs, send_vs, gsem = rest[12:]
    steps, rows, units = lo2.shape
    shard = rows // len(members)

    def in_copies(t):
        return [
            pltpu.make_async_copy(lo2h.at[t], lo2.at[t], lsem.at[0, t]),
            pltpu.make_async_copy(s2h.at[t], s2.at[t], lsem.at[1, t]),
        ]

    weight_copy = pltpu.make_async_copy(w2h, w2, wsem.at[0])
    below_copy = pltpu.make_async_copy(lo1h, lo1, wsem.at[1])
    for copy in in_copies(steps - 1):
        copy.start()
    weight_copy.start()
    for t in range(steps - 2, -1, -1):
        for copy in in_copies(t):
            copy.start()
    below_copy.start()

    lane = ROW0 + 16 - LANES
    valid_row = lanes - 1 - ROW0
    for n in tiles(units):
        total = st_own[:, n] + st_other[:, n]
        tail = st_own[:, units : units + LANES] + st_other[:, units : units + LANES]
        sums = tail[:, lanes - 1 : lanes]
        count = sums[valid_row : valid_row + 1]
        mean = total[valid_row : valid_row + 1] / count
        inv = lax.rsqrt(total[15:16] / count - mean * mean + 1e-05)
        head = wg[ROW0 : ROW0 + 16, n].astype(F32)
        sum_g = jnp.sum(head * sums, axis=0, keepdims=True)
        sum_gx = jnp.sum(head * total, axis=0, keepdims=True)
        slope = -0.5 * inv * inv * inv * (sum_gx - mean * sum_g)
        shift = -inv * sum_g - 2.0 * mean * slope
        coef[0:1, n] = mean
        coef[1:2, n] = inv
        coef[2:3, n] = shift / count
        coef[3:4, n] = 2.0 * slope / count
        gwo[:, n] = inv * (total - mean * sums)
        gwo[valid_row : valid_row + 1, n] = jnp.zeros_like(mean)
    gwo[:, units : units + LANES] = st_own[:, units : units + LANES] + st_other[:, units : units + LANES]

    def extra(t, n):
        packed = packs[t]
        valid = packed[:, lanes - 1 : lanes].astype(F32)
        grads = mm(packed, wg[:, n])
        values = lo2[t, :, n].astype(F32)
        result = coef[1:2, n] * grads + valid * (coef[2:3, n] + values * coef[3:4, n])
        return result.astype(BF16).astype(F32)

    def ready(t):
        for copy in in_copies(t):
            copy.wait()

    def out_copy(t):
        return pltpu.make_async_copy(dp2.at[t], dp2h.at[t], osem.at[t])

    last = steps - 1
    ready(last)
    for n in tiles(units):
        grad = extra(last, n)
        low = (grad * s2[last, :, n]).astype(BF16)
        dh[:, n] = grad
        bufa[:, n] = low
        dp2[last, :, n] = low
    out_copy(last).start()
    weight_copy.wait()
    back_steps(
        steps, dh, (bufa, bufb), dp2, w2,
        lambda n: rates[1:2, n],
        extra,
        lambda t, n: s2[t, :, n],
        ready,
        lambda t: out_copy(t).start(),
    )

    below_copy.wait()
    started = []
    if partners:
        me = lax.axis_index("wide")
        cols = [me] + [jnp.bitwise_xor(me, k) for k in partners]
        started += partial_grads(
            lo2, steps, 1, dp2, cols, width, own_w, sends, own_ws, send_ws, gsem.at[0], (w_a, w_b)
        )
        started += partial_grads(
            lo1, steps, 0, dp2, cols, width, own_v, sends, own_vs, send_vs, gsem.at[1], (v_a, v_b)
        )

    at = pl.ds(pl.multiple_of(own_rank(members) * shard, shard), shard)
    piece = steps // narrow
    who = lax.axis_index("narrow")
    for k in range(narrow):
        first = jnp.bitwise_xor(who, k) * piece
        for i in range(piece):
            values = lo2[first + i, at, :].astype(F32)
            normed = ((values - coef[0:1, :]) * coef[1:2, :]).astype(BF16)
            pieces[k, pl.ds(i * shard, shard), :] = mm_cols(normed, wg[...])
    for t in range(steps):
        out_copy(t).wait()
    for copy in started:
        copy.wait()


def back_one_kernel(members, partners, width, *refs):
    wx, rates, packs, dp2h, v2h, w1h, s1h, lo1h = refs[:8]
    inputs_out, dp1h = refs[8:10]
    rest = refs[10:]
    if partners:
        own_w, w_a, w_b, own_v, v_a = rest[:5]
        rest = rest[5:]
    (dp2, v2, dz, w1, s1, lo1, dp1, dh, bufa, bufb, vsem, lsem, wsem, osem) = rest[:14]
    if partners:
        sends, own_ws, send_ws, gsem = rest[14:]
    steps, rows, units = dz.shape
    shard = rows // len(members)

    first_copy = pltpu.make_async_copy(dp2h, dp2, wsem.at[0])
    first_copy.start()
    chunk = v2.shape[0] // vsem.shape[0]
    v_copies = [
        pltpu.make_async_copy(v2h.at[pl.ds(i * chunk, chunk)], v2.at[pl.ds(i * chunk, chunk)], vsem.at[i])
        for i in range(vsem.shape[0])
    ]
    for copy in v_copies:
        copy.start()
    slope_copies = [pltpu.make_async_copy(s1h.at[t], s1.at[t], lsem.at[t]) for t in range(steps)]
    weight_copy = pltpu.make_async_copy(w1h, w1, wsem.at[1])
    low_copy = pltpu.make_async_copy(lo1h, lo1, wsem.at[2])
    slope_copies[steps - 1].start()
    weight_copy.start()
    for t in range(steps - 2, -1, -1):
        slope_copies[t].start()
    low_copy.start()
    first_copy.wait()
    left = dp2[...].reshape(steps * rows, units)
    for i in range(vsem.shape[0]):
        v_copies[i].wait()
        part = mm_cols(dp2[...].reshape(steps * rows, units), v2[pl.ds(i * chunk, chunk), :])
        dz[:, :, pl.ds(i * chunk, chunk)] = part.reshape(steps, rows, chunk)

    def out_copy(t):
        return pltpu.make_async_copy(dp1.at[t], dp1h.at[t], osem.at[t])

    last = steps - 1
    slope_copies[last].wait()
    for n in tiles(units):
        grad = dz[last, :, n]
        low = (grad * s1[last, :, n]).astype(BF16)
        dh[:, n] = grad
        bufa[:, n] = low
        dp1[last, :, n] = low
    weight_copy.wait()
    for t in range(steps - 1):
        slope_copies[t].wait()
    back_steps(
        steps, dh, (bufa, bufb), dp1, w1,
        lambda n: rates[0:1, n],
        lambda t, n: dz[t, :, n],
        lambda t, n: s1[t, :, n],
        lambda t: None,
        lambda t: None,
    )
    low_copy.wait()
    if partners:
        me = lax.axis_index("wide")
        cols = [me] + [jnp.bitwise_xor(me, k) for k in partners]
        started = partial_grads(
            lo1, steps, 1, dp1, cols, width, own_w, sends, own_ws, send_ws, gsem.at[0], (w_a, w_b)
        )
        every = packs[...].reshape(steps * rows, LANES)
        for place, out in enumerate((own_v, v_a)):
            at = pl.ds(pl.multiple_of(cols[place] * width, LANES), width)
            part = mm_rows(every, dp1[:, :, at].reshape(steps * rows, width))
            out[...] = part.astype(out.dtype)
    else:
        started = [out_copy(t) for t in range(steps)]
        for copy in started:
            copy.start()
    at = pl.ds(pl.multiple_of(own_rank(members) * shard, shard), shard)
    part = mm_cols(dp1[:, at, :].reshape(steps * shard, units), wx[...])
    for t in range(steps):
        inputs_out[:, t, :] = part[t * shard : (t + 1) * shard]
    for copy in started:
        copy.wait()


def transpose_kernel(source, target):
    target[...] = source[...].T


def transposed(weight):
    size = weight.shape[0]
    return pl.pallas_call(
        transpose_kernel,
        grid=(size // 256,),
        in_specs=[pl.BlockSpec((256, size), lambda i: (i, 0))],
        out_specs=pl.BlockSpec((size, 256), lambda i: (0, i)),
        out_shape=jax.ShapeDtypeStruct((size, size), weight.dtype),
        cost_estimate=pl.CostEstimate(flops=0, bytes_accessed=4 * size * size, transcendentals=0),
        compiler_params=pltpu.CompilerParams(vmem_limit_bytes=16 << 20),
    )(weight)


def call(kernel, outs, out_specs, in_specs, scratch, flops, moved):
    return pl.pallas_call(
        kernel,
        out_shape=outs,
        in_specs=in_specs,
        out_specs=out_specs,
        scratch_shapes=scratch,
        cost_estimate=pl.CostEstimate(flops=flops, bytes_accessed=moved, transcendentals=0),
        compiler_params=pltpu.CompilerParams(vmem_limit_bytes=58 << 20),
    )


def on_device(
    inputs, cotangent, step_mask, washout, lengths, leak_groups, leak_two, w_one, v_one, v_two, w_two, w_out, b_out
):
    shard, steps, width_in = inputs.shape
    outputs = cotangent.shape[2]
    units = w_one.shape[1]
    wide, narrow = lax.axis_size("wide"), lax.axis_size("narrow")
    sets = max(wide // 4, 1)
    members = [d for d in range(wide) if set_of(d, sets) == 0]
    rows = shard * len(members)
    lanes = width_in + outputs + 1
    width = units // wide
    paired = sets == 2 and width % LANES == 0
    partners = (1, 2) if paired else ()
    shape = jax.ShapeDtypeStruct

    def across(x, axis, k):
        size = lax.axis_size(axis)
        return lax.ppermute(x, axis, [(i, i ^ k) for i in range(size)])

    position = jnp.arange(steps, dtype=jnp.int32)[None, :]
    valid = (step_mask == 1) & (position >= washout[:, None]) & (position < lengths[:, None])
    dy = jnp.where(valid[:, :, None], cotangent, jnp.zeros_like(cotangent))
    pack = jnp.concatenate(
        [inputs, dy, valid[:, :, None].astype(BF16), jnp.zeros((shard, steps, LANES - lanes), BF16)], axis=2
    )
    pack = jnp.transpose(pack, (1, 0, 2))
    blocks = [pack] + [across(pack, "wide", d) for d in members[1:]]
    w2t = transposed(w_two[0])
    w1t = transposed(w_one[0])

    wx = jnp.pad(v_one[0], ((0, LANES - width_in), (0, 0)))
    wg = jnp.pad(w_out.T, ((width_in, LANES - width_in - outputs), (0, 0)))
    rates = jnp.where(leak_groups[:, 0] == 0, F32(0.3), leak_two[0])

    unit = 2 * units * units
    low_t = shape((steps, rows, units), BF16)
    full_t = shape((steps, rows, units), F32)
    weight_s = pltpu.VMEM((units, units), BF16)
    low_s = pltpu.VMEM((steps, rows, units), BF16)
    full_s = pltpu.VMEM((steps, rows, units), F32)
    row_s = pltpu.VMEM((rows, units), BF16)
    state_s = pltpu.VMEM((rows, units), F32)
    dma = pltpu.SemaphoreType.DMA

    lo1, lo2, s1, s2, stats, packs = call(
        functools.partial(forward_kernel, members, lanes),
        [low_t, low_t, full_t, full_t, shape((16, units + LANES), F32), shape((steps, rows, LANES), BF16)],
        [ANY] * 4 + [VMEM] * 2,
        [VMEM] * (len(members) + 2) + [ANY] * 3,
        [weight_s] * 3 + [low_s] * 2 + [full_s] * 2 + [row_s] * 4 + [state_s] * 2
        + [pltpu.VMEM((8, units), F32), dma((3,)), dma((4, steps))],
        23 * rows * unit, 48 << 20,
    )(*blocks, wx, rates, w_one[0], v_two[0], w_two[0])

    k = 1
    while k * 2 < sets:
        stats = stats + across(stats, "wide", k)
        k *= 2
    other = across(stats, "wide", k) if sets > 1 else jnp.zeros_like(stats)

    own_t = shape((units, width), F32)
    send_t = shape((units // 2, width), BF16)
    grads_s = [
        pltpu.VMEM((units, width), F32),
        pltpu.VMEM((units, width), BF16),
    ]
    sends_s = pltpu.VMEM((steps * rows, 2 * width), BF16)
    piece = steps // narrow
    result = call(
        functools.partial(back_two_kernel, members, lanes, outputs, narrow, partners, width),
        [shape((narrow, piece * shard, LANES), F32), shape((16, units + LANES), F32), low_t]
        + [own_t, send_t, send_t] * (2 if paired else 0),
        [VMEM] * 2 + [ANY] * (7 if paired else 1),
        [VMEM] * 5 + [ANY] * 4,
        [low_s] * 2 + [full_s, weight_s, low_s, state_s, row_s, row_s, pltpu.VMEM((8, units), F32)]
        + [dma((2, steps)), dma((2,)), dma((steps,))]
        + ([sends_s] + grads_s * 2 + [dma((2, 3))] if paired else []),
        8 * rows * unit, 40 << 20,
    )(stats, other, wg, rates, packs, lo1, lo2, s2, w2t)
    pieces, gwo, dp2 = result[:3]

    result_one = call(
        functools.partial(back_one_kernel, members, partners, width),
        [shape((shard, steps, LANES), F32), low_t]
        + ([own_t, send_t, send_t, shape((LANES, width), F32), shape((LANES, width), F32)] if paired else []),
        [VMEM, ANY] + ([ANY] * 3 + [VMEM] * 2 if paired else []),
        [VMEM] * 3 + [ANY] * 5,
        [low_s, weight_s, full_s, weight_s, full_s, low_s, low_s, state_s, row_s, row_s]
        + [dma((8,)), dma((steps,)), dma((3,)), dma((steps,))]
        + ([sends_s] + grads_s + [dma((1, 3))] if paired else []),
        18 * rows * unit, 50 << 20,
    )(wx, rates, packs, dp2, v_two[0], w1t, s1, lo1)
    input_part, dp1 = result_one[:2]

    out = pieces[0]
    for k in range(1, narrow):
        out = out + across(pieces[k], "narrow", k)
    out = out[:, width_in : width_in + outputs].reshape(piece, shard, outputs) + b_out
    output = jnp.transpose(out, (1, 0, 2))

    k = 1
    while k < narrow:
        input_part = input_part + across(input_part, "narrow", k)
        k *= 2
    input_grad = input_part[:, :, :width_in]

    first = width_in - ROW0
    grad_w_out = gwo[first : first + outputs, :units].T
    grad_b_out = gwo[first : first + outputs, units + lanes - 1]

    if paired:

        def joined(own, a, b):
            got = jnp.concatenate([across(a, "wide", 1), across(b, "wide", 2)], axis=0)
            return own + got.astype(F32)

        grad_w_two = joined(*result[3:6])
        grad_v_two = joined(*result[6:9])
        grad_w_one = joined(*result_one[2:5])
        grad_v_one = (result_one[5] + across(result_one[6], "wide", 1))[:width_in]
    else:
        me = lax.axis_index("wide")
        rank = functools.reduce(lambda a, b: a + b, [((me ^ d) < me).astype(jnp.int32) for d in members[1:]])

        def own_rows(x):
            return lax.dynamic_slice_in_dim(x, rank * shard, shard, 1)

        def summed(left, right):
            part = jnp.einsum("tbr,tbq->rq", left, right, preferred_element_type=F32)
            return lax.psum_scatter(part, "wide", scatter_dimension=1, tiled=True)

        d1, d2, l1, l2, own = (own_rows(x) for x in (dp1, dp2, lo1, lo2, packs))
        grad_w_two = summed(l2[:-1], d2[1:])
        grad_v_two = summed(l1, d2)
        grad_w_one = summed(l1[:-1], d1[1:])
        grad_v_one = summed(own, d1)[:width_in]
    return (
        output,
        input_grad,
        grad_w_one[None],
        grad_v_one[None],
        grad_v_two[None],
        grad_w_two[None],
        grad_w_out,
        grad_b_out,
    )


def solution(mesh):
    in_specs = (
        P("wide", None, None),
        P("wide", None, None),
        P("wide", None),
        P("wide"),
        P("wide"),
        P(None, "narrow", None),
        P("narrow"),
        P("narrow", None, None),
        P("narrow", None, None),
        P("narrow", None, None),
        P("narrow", None, None),
        P("narrow", None),
        P(),
    )
    out_specs = (
        P("wide", "narrow", None),
        P("wide", None, None),
        P("narrow", None, "wide"),
        P("narrow", None, "wide"),
        P("narrow", None, "wide"),
        P("narrow", None, "wide"),
        P("narrow", None),
        P(),
    )
    return jax.shard_map(on_device, mesh=mesh, in_specs=in_specs, out_specs=out_specs, check_vma=False)
```

```python
import functools

import jax
import jax.numpy as jnp
from jax import lax
from jax.experimental import pallas as pl
from jax.experimental.pallas import tpu as pltpu
from jax.sharding import PartitionSpec as P

F32 = jnp.float32
BF16 = jnp.bfloat16
LANES = 128
ROW0 = 96
TILE = 512
VMEM = pl.BlockSpec(memory_space=pltpu.VMEM)
ANY = pl.BlockSpec(memory_space=pl.ANY)
ROWS_T = (((0,), (0,)), ((), ()))
COLS_T = (((1,), (1,)), ((), ()))


def mm(a, b):
    return jnp.dot(a, b, preferred_element_type=F32)


def mm_rows(a, b):
    return lax.dot_general(a, b, ROWS_T, preferred_element_type=F32)


def mm_cols(a, b):
    return lax.dot_general(a, b, COLS_T, preferred_element_type=F32)


def set_of(index, sets):
    return (index ^ (index >> 1)) & (sets - 1)


def tiles(width, tile=TILE):
    return [pl.ds(n, tile) for n in range(0, width, tile)]


def own_rank(members):
    me = lax.axis_index("wide")
    return functools.reduce(
        lambda a, b: a + b, [(jnp.bitwise_xor(me, d) < me).astype(jnp.int32) for d in members[1:]]
    )


def forward_kernel(members, lanes, *refs):
    blocks = refs[: len(members)]
    wx, rates, w1h, v2h, w2h = refs[len(members) : len(members) + 5]
    lo1h, lo2h, s1h, s2h, w1th, w2th, stats, packs = refs[len(members) + 5 : len(members) + 13]
    (w1, v2, w2, lo1, lo2, s1, s2, bufa, bufb, h1, ssq, flips, wsem, osem, fsem) = refs[len(members) + 13 :]
    steps, rows, units = lo1.shape
    shard = blocks[0].shape[1]

    def chunks(source, target, sems):
        return [
            pltpu.make_async_copy(source.at[:, n], target.at[:, n], sems.at[i])
            for i, n in enumerate(tiles(units))
        ]

    w1_in = chunks(w1h, w1, wsem.at[0])
    for copy in w1_in:
        copy.start()
    me = lax.axis_index("wide")
    for d, block in zip(members, blocks):
        rank = functools.reduce(
            lambda a, b: a + b,
            [
                (jnp.bitwise_xor(me, e) < jnp.bitwise_xor(me, d)).astype(jnp.int32)
                for e in members
                if e != d
            ],
            jnp.int32(0),
        )
        at = pl.ds(pl.multiple_of(rank * shard, shard), shard)
        for t in range(steps):
            packs[t, at, :] = block[t]
    ssq[...] = jnp.zeros_like(ssq)

    def layer_one(t, prev, new, arrive=None):
        for i, n in enumerate(tiles(units)):
            if arrive is not None:
                arrive[i].wait()
            acc = mm(packs[t], wx[:, n])
            if prev is not None:
                acc = acc + mm(prev[...], w1[:, n])
            th = jnp.tanh(acc)
            r = rates[0:1, n]
            if prev is None:
                h = r * th
            else:
                h = h1[:, n]
                h = h + r * (th - h)
            low = h.astype(BF16)
            h1[:, n] = h
            new[:, n] = low
            lo1[t, :, n] = low
            s1[t, :, n] = (r * (1.0 - th * th)).astype(s1.dtype)

    part = units // steps

    def flip_copy(i, t, slot):
        at = pl.ds(pl.multiple_of(t * part, part), part)
        return pltpu.make_async_copy(flips.at[slot, i], (w1th, w2th)[i].at[:, at], fsem.at[slot, i])

    def layer_two(t, prev, new, slot, reuse):
        valid = packs[t][:, lanes - 1 : lanes].astype(F32)
        at = pl.ds(pl.multiple_of(t * part, part), part)
        for i in range(2):
            if reuse:
                flip_copy(i, t - 2, slot).wait()
        for n in tiles(units):
            acc = mm(lo1[t], v2[:, n])
            if prev is not None:
                acc = acc + mm(prev[...], w2[:, n])
            flips[slot, 0, n, :] = w1[at, n].T
            flips[slot, 1, n, :] = w2[at, n].T
            th = jnp.tanh(acc)
            r = rates[1:2, n]
            if prev is None:
                h = r * th
            else:
                h = h1[:, n]
                h = h + r * (th - h)
            low = h.astype(BF16)
            h1[:, n] = h
            new[:, n] = low
            lo2[t, :, n] = low
            s2[t, :, n] = (r * (1.0 - th * th)).astype(s2.dtype)
            f = low.astype(F32)
            ssq[:, n] += jnp.sum((f * f * valid).reshape(rows // 8, 8, f.shape[1]), axis=0)
        for i in range(2):
            flip_copy(i, t, slot).start()
        for i in range(2):
            out_copy(i, t).start()

    def out_copy(i, t):
        src, dst = ((lo2, lo2h), (s2, s2h))[i]
        return pltpu.make_async_copy(src.at[t], dst.at[t], osem.at[i, t])

    v2_in = pltpu.make_async_copy(v2h, v2, wsem.at[1, 0])
    w2_in = pltpu.make_async_copy(w2h, w2, wsem.at[2, 0])
    lo1_out = pltpu.make_async_copy(lo1, lo1h, wsem.at[1, 1])
    s1_out = pltpu.make_async_copy(s1, s1h, wsem.at[2, 1])

    def pair_one(i, carry):
        t = 2 + 2 * i
        layer_one(t, bufb, bufa)
        layer_one(t + 1, bufa, bufb)
        return carry

    layer_one(0, None, bufa)
    layer_one(1, bufa, bufb, w1_in)
    v2_in.start()
    w2_in.start()
    lax.fori_loop(0, (steps - 2) // 2, pair_one, 0)
    lo1_out.start()
    s1_out.start()

    def pair_two(i, carry):
        t = 2 + 2 * i
        layer_two(t, bufb, bufa, 0, True)
        layer_two(t + 1, bufa, bufb, 1, True)
        return carry

    v2_in.wait()
    w2_in.wait()
    layer_two(0, None, bufa, 0, False)
    layer_two(1, bufa, bufb, 1, False)
    lax.fori_loop(0, (steps - 2) // 2, pair_two, 0)
    every = packs[...].reshape(steps * rows, LANES)
    for n in tiles(units):
        both = mm_rows(every, lo2[:, :, n].reshape(steps * rows, TILE))
        stats[:, n] = both[ROW0 : ROW0 + 16]
        stats[15:16, n] = jnp.sum(ssq[:, n], axis=0, keepdims=True)
    stats[:, units : units + LANES] = mm_rows(every, every)[ROW0 : ROW0 + 16]
    lo1_out.wait()
    s1_out.wait()
    for i in range(2):
        for t in range(steps):
            out_copy(i, t).wait()
        for slot in range(2):
            flip_copy(i, steps - 2 + slot, slot).wait()


def back_steps(steps, dh, bufs, dp_all, weight, rate_of, extra_of, slope_of, ready, done, arrive, then):
    units = dh.shape[1]

    def one(t, now, later, arrive=None):
        ready(t - 1)
        for i, n in enumerate(tiles(units)):
            if arrive is not None:
                arrive[i].wait()
            r = rate_of(n)
            grad = (1.0 - r) * dh[:, n] + mm(now[...], weight[:, n])
            grad = grad + extra_of(t - 1, n)
            low = (grad * slope_of(t - 1, n)).astype(BF16)
            dh[:, n] = grad
            later[:, n] = low
            dp_all[t - 1, :, n] = low
        done(t - 1)

    def pair(i, carry):
        t = steps - 2 - 2 * i
        one(t, bufs[1], bufs[0])
        one(t - 1, bufs[0], bufs[1])
        return carry

    one(steps - 1, bufs[0], bufs[1], arrive)
    for copy in then:
        copy.start()
    lax.fori_loop(0, (steps - 2) // 2, pair, 0)


def partial_grads(left, shift, dp_all, cols, width, right, stage, sems, outs):
    steps, rows, units = left.shape
    half = units // 2
    count = steps - shift
    started = []
    for side in range(2):
        at = pl.ds(pl.multiple_of(cols[1 + side] * width, LANES), width)
        right[side] = dp_all[:, :, at].reshape(steps * rows, width)
    for side in range(2):
        for m in range(0, half, TILE):
            at = pl.ds(side * half + m, TILE)
            l = left[:count, :, at].reshape(count * rows, TILE)
            stage[at, :] = mm_rows(l, right[side, shift * rows :, :]).astype(BF16)
        at = pl.ds(side * half, half)
        started.append(pltpu.make_async_copy(stage.at[at], outs[side], sems.at[side]))
        started[-1].start()
    return started


def back_two_kernel(members, lanes, partners, width, *refs):
    st_own, st_other, wg, rates, packs, lo1h, lo2h, s2h, w2h = refs[:9]
    readout, gwo, dp2h = refs[9:12]
    rest = refs[12:]
    if partners:
        own_cols, send_a, send_b = rest[:3]
        rest = rest[3:]
    (lo1, lo2, s2, w2, dp2, dh, bufa, bufb, coef, normed, lsem, wsem, osem) = rest[:13]
    if partners:
        right, send_ws, send_vs, gsem = rest[13:]
    steps, rows, units = lo2.shape
    shard = rows // len(members)

    def in_copies(t):
        return [
            pltpu.make_async_copy(lo2h.at[t], lo2.at[t], lsem.at[0, t]),
            pltpu.make_async_copy(s2h.at[t], s2.at[t], lsem.at[1, t]),
        ]

    weight_in = [
        pltpu.make_async_copy(w2h.at[:, n], w2.at[:, n], wsem.at[0, i]) for i, n in enumerate(tiles(units))
    ]
    below_in = pltpu.make_async_copy(lo1h, lo1, wsem.at[1, 0])
    for copy in in_copies(steps - 1) + weight_in[:1] + in_copies(steps - 2) + weight_in[1:]:
        copy.start()

    valid_row = lanes - 1 - ROW0
    for n in tiles(units):
        total = st_own[:, n] + st_other[:, n]
        tail = st_own[:, units : units + LANES] + st_other[:, units : units + LANES]
        sums = tail[:, lanes - 1 : lanes]
        count = sums[valid_row : valid_row + 1]
        mean = total[valid_row : valid_row + 1] / count
        inv = lax.rsqrt(total[15:16] / count - mean * mean + 1e-05)
        head = wg[ROW0 : ROW0 + 16, n].astype(F32)
        sum_g = jnp.sum(head * sums, axis=0, keepdims=True)
        sum_gx = jnp.sum(head * total, axis=0, keepdims=True)
        slope = -0.5 * inv * inv * inv * (sum_gx - mean * sum_g)
        shift = -inv * sum_g - 2.0 * mean * slope
        coef[0:1, n] = mean
        coef[1:2, n] = inv
        coef[2:3, n] = shift / count
        coef[3:4, n] = 2.0 * slope / count
        gwo[:, n] = inv * (total - mean * sums)
        gwo[valid_row : valid_row + 1, n] = jnp.zeros_like(mean)
    gwo[:, units : units + LANES] = st_own[:, units : units + LANES] + st_other[:, units : units + LANES]

    def extra(t, n):
        packed = packs[t]
        valid = packed[:, lanes - 1 : lanes].astype(F32)
        grads = mm(packed, wg[:, n])
        values = lo2[t, :, n].astype(F32)
        result = coef[1:2, n] * grads + valid * (coef[2:3, n] + values * coef[3:4, n])
        return result.astype(BF16).astype(F32)

    def ready(t):
        for copy in in_copies(t):
            copy.wait()

    def out_copy(t):
        return pltpu.make_async_copy(dp2.at[t], dp2h.at[t], osem.at[t])

    last = steps - 1
    ready(last)
    for n in tiles(units):
        grad = extra(last, n)
        low = (grad * s2[last, :, n]).astype(BF16)
        dh[:, n] = grad
        bufa[:, n] = low
        dp2[last, :, n] = low
    out_copy(last).start()
    later = [copy for t in range(steps - 3, -1, -1) for copy in in_copies(t)]
    back_steps(
        steps, dh, (bufa, bufb), dp2, w2,
        lambda n: rates[1:2, n],
        extra,
        lambda t, n: s2[t, :, n],
        ready,
        lambda t: out_copy(t).start(),
        weight_in,
        later + [below_in],
    )

    below_in.wait()
    started = []
    if partners:
        me = lax.axis_index("wide")
        cols = [me] + [jnp.bitwise_xor(me, k) for k in partners]
        half = pl.ds(0, units // 2)
        outs = (send_a.at[half], send_b.at[half])
        started += partial_grads(lo2, 1, dp2, cols, width, right, send_ws, gsem.at[0], outs)
        half = pl.ds(units // 2, units // 2)
        outs = (send_a.at[half], send_b.at[half])
        started += partial_grads(lo1, 0, dp2, cols, width, right, send_vs, gsem.at[1], outs)
        own_cols[...] = dp2[:, :, pl.ds(pl.multiple_of(me * width, LANES), width)]

    at = pl.ds(pl.multiple_of(own_rank(members) * shard, shard), shard)
    for n in tiles(units):
        values = lo2[:, at, n].astype(F32).reshape(steps * shard, TILE)
        normed[:, n] = ((values - coef[0:1, n]) * coef[1:2, n]).astype(BF16)
    part = mm_cols(normed[...], wg[...])
    for t in range(steps):
        readout[:, t, :] = part[t * shard : (t + 1) * shard]
    for t in range(steps):
        out_copy(t).wait()
    for copy in started:
        copy.wait()


def back_one_kernel(members, partners, width, *refs):
    wx, rates, packs, readout, dp2h, v2h, w1h, s1h, lo1h = refs[:9]
    combined, dp1h = refs[9:11]
    rest = refs[11:]
    if partners:
        own_cols, own_v, send_a, send_b = rest[:4]
        rest = rest[4:]
    (dp2, v2, dz, w1, s1, lo1, dp1, dh, bufa, bufb, vsem, lsem, wsem, osem) = rest[:14]
    if partners:
        right, send_ws, v_stage, gsem = rest[14:]
    steps, rows, units = dz.shape
    shard = rows // len(members)
    pieces = [pl.ds(0, units // 4), pl.ds(units // 4, units // 4), pl.ds(units // 2, units // 2)]
    first_in = pltpu.make_async_copy(dp2h, dp2, wsem.at[1, 0])
    low_in = pltpu.make_async_copy(lo1h, lo1, wsem.at[1, 1])
    v_in = [pltpu.make_async_copy(v2h.at[n], v2.at[n], vsem.at[i]) for i, n in enumerate(pieces)]
    slope_in = pltpu.make_async_copy(s1h, s1, lsem.at[0])
    weight_in = pltpu.make_async_copy(w1h, w1, wsem.at[0, 0])
    for copy in [first_in] + v_in:
        copy.start()
    first_in.wait()
    for i, n in enumerate(pieces):
        v_in[i].wait()
        if i == 1:
            slope_in.start()
            weight_in.start()
            low_in.start()
        part = mm_cols(dp2[...].reshape(steps * rows, units), v2[n, :])
        dz[:, :, n] = part.reshape(steps, rows, n.size)

    def out_copy(t):
        return pltpu.make_async_copy(dp1.at[t], dp1h.at[t], osem.at[t])

    last = steps - 1
    slope_in.wait()
    weight_in.wait()
    for n in tiles(units):
        grad = dz[last, :, n]
        low = (grad * s1[last, :, n]).astype(BF16)
        dh[:, n] = grad
        bufa[:, n] = low
        dp1[last, :, n] = low
    back_steps(
        steps, dh, (bufa, bufb), dp1, w1,
        lambda n: rates[0:1, n],
        lambda t, n: dz[t, :, n],
        lambda t, n: s1[t, :, n],
        lambda t: None,
        lambda t: None,
        None,
        (),
    )
    low_in.wait()
    if partners:
        me = lax.axis_index("wide")
        cols = [me] + [jnp.bitwise_xor(me, k) for k in partners]
        half = units // 2
        outs = (send_a.at[pl.ds(0, half)], send_b)
        started = partial_grads(lo1, 1, dp1, cols, width, right, send_ws, gsem, outs)
        own_cols[...] = dp1[:, :, pl.ds(pl.multiple_of(me * width, LANES), width)]
        every = packs[...].reshape(steps * rows, LANES)
        for place in range(2):
            at = pl.ds(pl.multiple_of(cols[place] * width, LANES), width)
            part = mm_rows(every, dp1[:, :, at].reshape(steps * rows, width))
            if place == 0:
                own_v[...] = part
            else:
                v_stage[...] = part.astype(BF16)
        started.append(pltpu.make_async_copy(v_stage, send_a.at[pl.ds(half, LANES)], wsem.at[1, 2]))
        started[-1].start()
    else:
        started = [out_copy(t) for t in range(steps)]
        for copy in started:
            copy.start()
    at = pl.ds(pl.multiple_of(own_rank(members) * shard, shard), shard)
    part = mm_cols(dp1[:, at, :].reshape(steps * shard, units), wx[...])
    for t in range(steps):
        combined[:, t, :] = readout[:, t, :] + part[t * shard : (t + 1) * shard]
    for copy in started:
        copy.wait()


def own_kernel(lo1, lo2, dp1, dp2, wa, va, wb, vb, w_two, v_two, w_one):
    steps, rows, width = dp2.shape
    tile = lo1.shape[2]
    side = pl.program_id(0)
    got_w = jnp.where(side == 0, wa[...], wb[...]).astype(F32)
    got_v = jnp.where(side == 0, va[...], vb[...]).astype(F32)

    def product(left, right, shift):
        count = steps - shift
        return mm_rows(left[:count].reshape(count * rows, tile), right[shift:].reshape(count * rows, width))

    w_two[...] = got_w + product(lo2, dp2, 1)
    v_two[...] = got_v + product(lo1, dp2, 0)
    w_one[...] = product(lo1, dp1, 1)


def own_columns(lo1, lo2, dp1, dp2, got_a, got_b):
    steps, rows, units = lo1.shape
    width = dp1.shape[2]
    many = units // 2 // TILE
    low = pl.BlockSpec((steps, rows, TILE), lambda s, m: (0, 0, s * many + m))
    dp = pl.BlockSpec((steps, rows, width), lambda s, m: (0, 0, 0))
    got = [
        pl.BlockSpec((TILE, width), functools.partial(lambda a, b, s, m: (b + jnp.where(s == a, m, 0), 0), a, b))
        for a, b in ((0, 0), (0, many), (1, 0), (1, many))
    ]
    out = pl.BlockSpec((TILE, width), lambda s, m: (s * many + m, 0))
    return pl.pallas_call(
        own_kernel,
        grid=(2, many),
        in_specs=[low, low, dp, dp] + got,
        out_specs=[out] * 3,
        out_shape=[jax.ShapeDtypeStruct((units, width), F32)] * 3,
        cost_estimate=pl.CostEstimate(
            flops=6 * steps * rows * units * width, bytes_accessed=17 << 20, transcendentals=0
        ),
        compiler_params=pltpu.CompilerParams(vmem_limit_bytes=60 << 20),
    )(lo1, lo2, dp1, dp2, got_a, got_a, got_b, got_b)


def call(kernel, outs, out_specs, in_specs, scratch, flops, moved, mib):
    return pl.pallas_call(
        kernel,
        out_shape=outs,
        in_specs=in_specs,
        out_specs=out_specs,
        scratch_shapes=scratch,
        cost_estimate=pl.CostEstimate(flops=flops, bytes_accessed=moved, transcendentals=0),
        compiler_params=pltpu.CompilerParams(vmem_limit_bytes=mib << 20),
    )


def on_device(
    inputs, cotangent, step_mask, washout, lengths, leak_groups, leak_two, w_one, v_one, v_two, w_two, w_out, b_out
):
    shard, steps, width_in = inputs.shape
    outputs = cotangent.shape[2]
    units = w_one.shape[1]
    wide, narrow = lax.axis_size("wide"), lax.axis_size("narrow")
    sets = max(wide // 4, 1)
    members = [d for d in range(wide) if set_of(d, sets) == 0]
    rows = shard * len(members)
    lanes = width_in + outputs + 1
    width = units // wide
    paired = sets == 2 and width % LANES == 0
    partners = (1, 2) if paired else ()
    shape = jax.ShapeDtypeStruct

    def across(x, axis, k):
        size = lax.axis_size(axis)
        return lax.ppermute(x, axis, [(i, i ^ k) for i in range(size)])

    position = jnp.arange(steps, dtype=jnp.int32)[None, :]
    valid = (step_mask == 1) & (position >= washout[:, None]) & (position < lengths[:, None])
    dy = jnp.where(valid[:, :, None], cotangent, jnp.zeros_like(cotangent))
    pack = jnp.concatenate(
        [inputs, dy, valid[:, :, None].astype(BF16), jnp.zeros((shard, steps, LANES - lanes), BF16)], axis=2
    )
    pack = jnp.transpose(pack, (1, 0, 2))
    blocks = [pack] + [across(pack, "wide", d) for d in members[1:]]

    wx = jnp.pad(v_one[0], ((0, LANES - width_in), (0, 0)))
    wg = jnp.pad(w_out.T, ((width_in, LANES - width_in - outputs), (0, 0)))
    rates = jnp.where(leak_groups[:, 0] == 0, F32(0.3), leak_two[0])

    unit = 2 * units * units
    low_t = shape((steps, rows, units), BF16)
    weight_s = pltpu.VMEM((units, units), BF16)
    low_s = pltpu.VMEM((steps, rows, units), BF16)
    full_s = pltpu.VMEM((steps, rows, units), F32)
    row_s = pltpu.VMEM((rows, units), BF16)
    state_s = pltpu.VMEM((rows, units), F32)
    dma = pltpu.SemaphoreType.DMA

    weight_t = shape((units, units), BF16)
    lo1, lo2, s1, s2, w1t, w2t, stats, packs = call(
        functools.partial(forward_kernel, members, lanes),
        [low_t] * 4 + [weight_t] * 2 + [shape((16, units + LANES), F32), shape((steps, rows, LANES), BF16)],
        [ANY] * 6 + [VMEM] * 2,
        [VMEM] * (len(members) + 2) + [ANY] * 3,
        [weight_s] * 3 + [low_s] * 4 + [row_s] * 2 + [state_s]
        + [pltpu.VMEM((8, units), F32), pltpu.VMEM((2, 2, units, units // steps), BF16)]
        + [dma((3, units // TILE)), dma((2, steps)), dma((2, 2))],
        23 * rows * unit, 48 << 20, 60,
    )(*blocks, wx, rates, w_one[0], v_two[0], w_two[0])

    k = 1
    while k * 2 < sets:
        stats = stats + across(stats, "wide", k)
        k *= 2
    other = across(stats, "wide", k) if sets > 1 else jnp.zeros_like(stats)

    cols_t = shape((steps, rows, width), BF16)
    right_s = pltpu.VMEM((2, steps * rows, width), BF16)
    grads_s = pltpu.VMEM((units, width), BF16)
    chunk_n = units // TILE
    result = call(
        functools.partial(back_two_kernel, members, lanes, partners, width),
        [shape((shard, steps, LANES), F32), shape((16, units + LANES), F32), low_t]
        + ([cols_t] + [shape((units, width), BF16)] * 2 if paired else []),
        [VMEM] * 2 + [ANY] + ([VMEM, ANY, ANY] if paired else []),
        [VMEM] * 5 + [ANY] * 4,
        [low_s] * 3 + [weight_s, low_s, state_s, row_s, row_s, pltpu.VMEM((8, units), F32)]
        + [pltpu.VMEM((steps * shard, units), BF16), dma((2, steps)), dma((2, chunk_n)), dma((steps,))]
        + ([right_s, grads_s, grads_s, dma((2, 2))] if paired else []),
        8 * rows * unit, 40 << 20, 60,
    )(stats, other, wg, rates, packs, lo1, lo2, s2, w2t)
    readout, gwo, dp2 = result[:3]

    result_one = call(
        functools.partial(back_one_kernel, members, partners, width),
        [shape((shard, steps, LANES), F32), low_t]
        + ([cols_t, shape((LANES, width), F32)] if paired else [])
        + ([shape((units // 2 + LANES, width), BF16), shape((units // 2, width), BF16)] if paired else []),
        [VMEM, ANY] + ([VMEM, VMEM, ANY, ANY] if paired else []),
        [VMEM] * 4 + [ANY] * 5,
        [low_s, weight_s, full_s, weight_s, low_s, low_s, low_s, state_s, row_s, row_s]
        + [dma((8,)), dma((steps,)), dma((2, chunk_n)), dma((steps,))]
        + ([right_s, grads_s, pltpu.VMEM((LANES, width), BF16), dma((2,))] if paired else []),
        18 * rows * unit, 50 << 20, 60,
    )(wx, rates, packs, readout, dp2, v_two[0], w1t, s1, lo1)
    combined, dp1 = result_one[:2]

    k = 1
    while k < narrow:
        combined = combined + across(combined, "narrow", k)
        k *= 2
    input_grad = combined[:, :, :width_in]
    piece = steps // narrow
    mine = lax.dynamic_slice_in_dim(combined, lax.axis_index("narrow") * piece, piece, 1)
    output = mine[:, :, width_in : width_in + outputs] + b_out

    first = width_in - ROW0
    grad_w_out = gwo[first : first + outputs, :units].T
    grad_b_out = gwo[first : first + outputs, units + lanes - 1]

    if paired:

        half = units // 2
        cols_two, send_a, send_b = result[3:]
        got_a, got_b = across(send_a, "wide", 1), across(send_b, "wide", 2)
        cols_one, own_v1, send_a, send_b = result_one[2:]
        got_a, got_b, send_a, send_b = lax.optimization_barrier((got_a, got_b, send_a, send_b))
        grad_w_two, grad_v_two, own_w1 = own_columns(lo1, lo2, cols_one, cols_two, got_a, got_b)
        got_a, got_b = across(send_a, "wide", 1), across(send_b, "wide", 2)
        grad_w_one = own_w1 + jnp.concatenate([got_a[:half], got_b], axis=0).astype(F32)
        grad_v_one = (own_v1 + got_a[half:].astype(F32))[:width_in]
    else:
        me = lax.axis_index("wide")
        rank = functools.reduce(lambda a, b: a + b, [((me ^ d) < me).astype(jnp.int32) for d in members[1:]])

        def own_rows(x):
            return lax.dynamic_slice_in_dim(x, rank * shard, shard, 1)

        def summed(left, right):
            part = jnp.einsum("tbr,tbq->rq", left, right, preferred_element_type=F32)
            return lax.psum_scatter(part, "wide", scatter_dimension=1, tiled=True)

        d1, d2, l1, l2, own = (own_rows(x) for x in (dp1, dp2, lo1, lo2, packs))
        grad_w_two = summed(l2[:-1], d2[1:])
        grad_v_two = summed(l1, d2)
        grad_w_one = summed(l1[:-1], d1[1:])
        grad_v_one = summed(own, d1)[:width_in]
    return (
        output,
        input_grad,
        grad_w_one[None],
        grad_v_one[None],
        grad_v_two[None],
        grad_w_two[None],
        grad_w_out,
        grad_b_out,
    )


def solution(mesh):
    in_specs = (
        P("wide", None, None),
        P("wide", None, None),
        P("wide", None),
        P("wide"),
        P("wide"),
        P(None, "narrow", None),
        P("narrow"),
        P("narrow", None, None),
        P("narrow", None, None),
        P("narrow", None, None),
        P("narrow", None, None),
        P("narrow", None),
        P(),
    )
    out_specs = (
        P("wide", "narrow", None),
        P("wide", None, None),
        P("narrow", None, "wide"),
        P("narrow", None, "wide"),
        P("narrow", None, "wide"),
        P("narrow", None, "wide"),
        P("narrow", None),
        P(),
    )
    return jax.shard_map(on_device, mesh=mesh, in_specs=in_specs, out_specs=out_specs, check_vma=False)
```

```python
import functools

import jax
import jax.numpy as jnp
from jax import lax
from jax.experimental import pallas as pl
from jax.experimental.pallas import tpu as pltpu
from jax.sharding import PartitionSpec as P

F32 = jnp.float32
BF16 = jnp.bfloat16
SLOPE = F32
JOIN = 24
LANES = 128
ROW0 = 96
TILE = 512
VMEM = pl.BlockSpec(memory_space=pltpu.VMEM)
ANY = pl.BlockSpec(memory_space=pl.ANY)
ROWS_T = (((0,), (0,)), ((), ()))
COLS_T = (((1,), (1,)), ((), ()))


def mm(a, b):
    return jnp.dot(a, b, preferred_element_type=F32)


def mm_rows(a, b):
    return lax.dot_general(a, b, ROWS_T, preferred_element_type=F32)


def mm_cols(a, b):
    return lax.dot_general(a, b, COLS_T, preferred_element_type=F32)


def set_of(index, sets):
    return (index ^ (index >> 1)) & (sets - 1)


def tiles(width, tile=TILE):
    return [pl.ds(n, tile) for n in range(0, width, tile)]


def own_rank(members):
    me = lax.axis_index("wide")
    return functools.reduce(
        lambda a, b: a + b, [(jnp.bitwise_xor(me, d) < me).astype(jnp.int32) for d in members[1:]]
    )


def forward_kernel(members, lanes, small, *refs):
    blocks = refs[: len(members)]
    wx, rates, w1h, v2h, w2h = refs[len(members) : len(members) + 5]
    lo1h, lo2h, s1h, s2h, w1th, w2th, stats, packs = refs[len(members) + 5 : len(members) + 13]
    (w1, v2, w2, lo1, lo2, s1, s2, bufa, bufb, h1, ssq, flips, turn, wsem, osem, fsem) = refs[len(members) + 13 :]
    steps, rows, units = lo1.shape
    shard = blocks[0].shape[0]

    def chunks(source, target, sems):
        return [
            pltpu.make_async_copy(source.at[:, n], target.at[:, n], sems.at[i])
            for i, n in enumerate(tiles(units))
        ]

    w1_in = chunks(w1h, w1, wsem.at[0])
    for copy in w1_in:
        copy.start()
    small.ready()
    me = lax.axis_index("wide")
    for d, block in zip(members, blocks):
        rank = functools.reduce(
            lambda a, b: a + b,
            [
                (jnp.bitwise_xor(me, e) < jnp.bitwise_xor(me, d)).astype(jnp.int32)
                for e in members
                if e != d
            ],
            jnp.int32(0),
        )
        at = pl.ds(pl.multiple_of(rank * shard, shard), shard)
        turn[...] = block[...].astype(F32)
        for t in range(steps):
            packs[t, at, :] = turn[:, t, :].astype(BF16)
    small.flush(packs)
    ssq[...] = jnp.zeros_like(ssq)

    def layer_one(t, prev, new, arrive=None):
        for i, n in enumerate(tiles(units)):
            if arrive is not None:
                arrive[i].wait()
            acc = mm(packs[t], wx[:, n])
            if prev is not None:
                acc = acc + mm(prev[...], w1[:, n])
            th = jnp.tanh(acc)
            r = rates[0:1, n]
            if prev is None:
                h = r * th
            else:
                h = h1[:, n]
                h = h + r * (th - h)
            low = h.astype(BF16)
            h1[:, n] = h
            new[:, n] = low
            lo1[t, :, n] = low
            s1[t, :, n] = (r * (1.0 - th * th)).astype(s1.dtype)

    part = units // steps

    def flip_copies(t, slot):
        at = pl.ds(pl.multiple_of(t * part, part), part)
        return [
            pltpu.make_async_copy(flips.at[slot, i], out.at[:, at], fsem.at[slot, i])
            for i, out in enumerate((w1th, w2th))
        ]

    def layer_two(t, prev, new, slot):
        valid = packs[t][:, lanes - 1 : lanes].astype(F32)
        at = pl.ds(pl.multiple_of(t * part, part), part)
        for n in tiles(units):
            acc = mm(lo1[t], v2[:, n])
            if prev is not None:
                acc = acc + mm(prev[...], w2[:, n])
            flips[slot, 0, n, :] = w1[at, n].T
            flips[slot, 1, n, :] = w2[at, n].T
            th = jnp.tanh(acc)
            r = rates[1:2, n]
            if prev is None:
                h = r * th
            else:
                h = h1[:, n]
                h = h + r * (th - h)
            low = h.astype(BF16)
            h1[:, n] = h
            new[:, n] = low
            lo2[t, :, n] = low
            s2[t, :, n] = (r * (1.0 - th * th)).astype(s2.dtype)
            f = low.astype(F32)
            ssq[:, n] += jnp.sum((f * f * valid).reshape(rows // 8, 8, f.shape[1]), axis=0)

    def out_copies(t):
        return [
            pltpu.make_async_copy(src.at[t], dst.at[t], osem.at[i, t])
            for i, (src, dst) in enumerate(((lo2, lo2h), (s2, s2h)))
        ]

    v2_in = pltpu.make_async_copy(v2h, v2, wsem.at[1, 0])
    w2_in = pltpu.make_async_copy(w2h, w2, wsem.at[2, 0])
    lo1_out = pltpu.make_async_copy(lo1, lo1h, wsem.at[1, 1])
    s1_out = pltpu.make_async_copy(s1, s1h, wsem.at[2, 1])

    def pair_one(i, carry):
        t = 2 + 2 * i
        layer_one(t, bufb, bufa)
        layer_one(t + 1, bufa, bufb)
        return carry

    layer_one(0, None, bufa)
    layer_one(1, bufa, bufb, w1_in)
    v2_in.start()
    w2_in.start()
    lax.fori_loop(0, (steps - 2) // 2, pair_one, 0)
    lo1_out.start()
    s1_out.start()

    def step_two(t, prev, new, slot, reuse):
        if reuse:
            for copy in flip_copies(t - 2, slot):
                copy.wait()
        layer_two(t, prev, new, slot)
        for copy in flip_copies(t, slot) + out_copies(t):
            copy.start()

    def pair_two(i, carry):
        t = 2 + 2 * i
        step_two(t, bufb, bufa, 0, True)
        step_two(t + 1, bufa, bufb, 1, True)
        return carry

    v2_in.wait()
    w2_in.wait()
    step_two(0, None, bufa, 0, False)
    step_two(1, bufa, bufb, 1, False)
    lax.fori_loop(0, (steps - 2) // 2, pair_two, 0)
    every = packs[...].reshape(steps * rows, LANES)
    for n in tiles(units):
        both = mm_rows(every, lo2[:, :, n].reshape(steps * rows, TILE))
        stats[:, n] = both[ROW0 : ROW0 + 16]
        stats[15:16, n] = jnp.sum(ssq[:, n], axis=0, keepdims=True)
    stats[:, units : units + LANES] = mm_rows(every, every)[ROW0 : ROW0 + 16]
    small.flush(stats)
    lo1_out.wait()
    s1_out.wait()
    for t in range(steps):
        for copy in out_copies(t):
            copy.wait()
    for slot in range(2):
        for copy in flip_copies(steps - 2 + slot, slot):
            copy.wait()


def back_steps(steps, dh, bufs, dp_all, weight, rate_of, extra, slope, weight_in, slope_in):
    units = dh.shape[1]

    def one(t, now, later, arrive=None):
        for i, n in enumerate(tiles(units)):
            if arrive is not None:
                arrive[i].wait()
            r = rate_of(n)
            grad = (1.0 - r) * dh[:, n] + mm(now[...], weight[:, n])
            grad = grad + extra[t - 1, :, n].astype(F32)
            low = (grad * slope[t - 1, :, n].astype(F32)).astype(BF16)
            dh[:, n] = grad
            later[:, n] = low
            dp_all[t - 1, :, n] = low

    def pair(i, carry):
        t = steps - 2 - 2 * i
        one(t, bufs[1], bufs[0])
        one(t - 1, bufs[0], bufs[1])
        return carry

    for n in tiles(units):
        grad = extra[steps - 1, :, n].astype(F32)
        low = (grad * slope[steps - 1, :, n].astype(F32)).astype(BF16)
        dh[:, n] = grad
        bufs[0][:, n] = low
        dp_all[steps - 1, :, n] = low
    one(steps - 1, bufs[0], bufs[1], weight_in)
    if slope_in is not None:
        slope_in.wait()
    lax.fori_loop(0, (steps - 2) // 2, pair, 0)


def partial_grads(left, shift, dp_all, cols, width, right, stage, sems, outs):
    steps, rows, units = left.shape
    half = units // 2
    count = steps - shift
    started = []
    for side in range(2):
        at = pl.ds(pl.multiple_of(cols[1 + side] * width, LANES), width)
        right[side] = dp_all[:, :, at].reshape(steps * rows, width)
    for side in range(2):
        for m in range(0, half, TILE):
            at = pl.ds(side * half + m, TILE)
            l = left[:count, :, at].reshape(count * rows, TILE)
            stage[at, :] = mm_rows(l, right[side, shift * rows :, :]).astype(BF16)
        at = pl.ds(side * half, half)
        started.append(pltpu.make_async_copy(stage.at[at], outs[side], sems.at[side]))
        started[-1].start()
    return started


def back_two_kernel(members, lanes, partners, width, small, *refs):
    st_own, st_other, wg, rates, packs, lo1h, lo2h, s2h, w2h = refs[:9]
    readout, gwo, gbo, dp2h = refs[9:13]
    rest = refs[13:]
    if partners:
        own_cols, send_a, send_b = rest[:3]
        rest = rest[3:]
    (lo1, lo2, s2, w2, dp2, dfeat, dh, bufa, bufb, coef, normed, wsem) = rest[:12]
    if partners:
        right, send_ws, send_vs, gsem = rest[12:]
    steps, rows, units = lo2.shape
    shard = rows // len(members)
    lo2_in = pltpu.make_async_copy(lo2h, lo2, wsem.at[0])
    last = pl.ds(steps - 2, 2)
    rest_of = pl.ds(0, steps - 2)
    s2_last = pltpu.make_async_copy(s2h.at[last], s2.at[last], wsem.at[1])
    s2_in = pltpu.make_async_copy(s2h.at[rest_of], s2.at[rest_of], wsem.at[5])
    w2_in = [pltpu.make_async_copy(w2h.at[:, n], w2.at[:, n], wsem.at[6 + i]) for i, n in enumerate(tiles(units))]
    lo1_in = pltpu.make_async_copy(lo1h, lo1, wsem.at[3])
    dp2_out = pltpu.make_async_copy(dp2, dp2h, wsem.at[4])
    small.ready()
    for copy in (lo2_in, s2_last, *w2_in):
        copy.start()

    valid_row = lanes - 1 - ROW0
    for n in tiles(units):
        total = st_own[:, n] + st_other[:, n]
        tail = st_own[:, units : units + LANES] + st_other[:, units : units + LANES]
        sums = tail[:, lanes - 1 : lanes]
        count = sums[valid_row : valid_row + 1]
        mean = total[valid_row : valid_row + 1] / count
        inv = lax.rsqrt(total[15:16] / count - mean * mean + 1e-05)
        head = wg[ROW0 : ROW0 + 16, n].astype(F32)
        sum_g = jnp.sum(head * sums, axis=0, keepdims=True)
        sum_gx = jnp.sum(head * total, axis=0, keepdims=True)
        slope = -0.5 * inv * inv * inv * (sum_gx - mean * sum_g)
        shift = -inv * sum_g - 2.0 * mean * slope
        coef[0:1, n] = mean
        coef[1:2, n] = inv
        coef[2:3, n] = shift / count
        coef[3:4, n] = 2.0 * slope / count
        first = valid_row - gwo.shape[0]
        gwo[:, n] = (inv * (total - mean * sums))[first:valid_row]
        gbo[...] = tail[valid_row : valid_row + 1, lanes - 1 - gbo.shape[1] : lanes - 1]

    small.flush(gwo)
    small.flush(gbo)
    lo2_in.wait()
    s2_in.start()
    lo1_in.start()

    def feature_grads(t, carry):
        packed = packs[t]
        valid = packed[:, lanes - 1 : lanes].astype(F32)
        for n in tiles(units):
            grads = mm(packed, wg[:, n])
            values = lo2[t, :, n].astype(F32)
            result = coef[1:2, n] * grads + valid * (coef[2:3, n] + values * coef[3:4, n])
            dfeat[t, :, n] = result.astype(BF16)
        return carry

    lax.fori_loop(0, steps, feature_grads, 0)
    s2_last.wait()
    back_steps(steps, dh, (bufa, bufb), dp2, w2, lambda n: rates[1:2, n], dfeat, s2, w2_in, s2_in)
    dp2_out.start()
    lo1_in.wait()
    started = []
    if partners:
        me = lax.axis_index("wide")
        cols = [me] + [jnp.bitwise_xor(me, k) for k in partners]
        half = pl.ds(0, units // 2)
        outs = (send_a.at[half], send_b.at[half])
        started += partial_grads(lo2, 1, dp2, cols, width, right, send_ws, gsem.at[0], outs)
        half = pl.ds(units // 2, units // 2)
        outs = (send_a.at[half], send_b.at[half])
        started += partial_grads(lo1, 0, dp2, cols, width, right, send_vs, gsem.at[1], outs)
        own_cols[...] = dp2[:, :, pl.ds(pl.multiple_of(me * width, LANES), width)]
        small.flush(own_cols)

    at = pl.ds(pl.multiple_of(own_rank(members) * shard, shard), shard)
    for n in tiles(units):
        values = lo2[:, at, n].astype(F32).reshape(steps * shard, TILE)
        normed[:, n] = ((values - coef[0:1, n]) * coef[1:2, n]).astype(BF16)
    part = mm_cols(normed[...], wg[...])
    for t in range(steps):
        readout[:, t, :] = part[t * shard : (t + 1) * shard]
    small.flush(readout)
    dp2_out.wait()
    for copy in started:
        copy.wait()


def back_one_kernel(members, partners, width, small, *refs):
    wx, rates, packs, readout, dp2h, v2h, w1h, s1h, lo1h = refs[:9]
    combined, dp1h = refs[9:11]
    rest = refs[11:]
    if partners:
        own_cols, own_v, send_a, send_b = rest[:4]
        rest = rest[4:]
    (dp2, v2, dz, w1, s1, lo1, dp1, dh, bufa, bufb, vsem, lsem, wsem, osem) = rest[:14]
    if partners:
        right, send_ws, v_stage, gsem = rest[14:]
    steps, rows, units = dz.shape
    shard = rows // len(members)
    pieces = [pl.ds(0, units // 4), pl.ds(units // 4, units // 4), pl.ds(units // 2, units // 2)]
    first_in = pltpu.make_async_copy(dp2h, dp2, wsem.at[1, 0])
    low_in = pltpu.make_async_copy(lo1h, lo1, wsem.at[1, 1])
    v_in = [pltpu.make_async_copy(v2h.at[n], v2.at[n], vsem.at[i]) for i, n in enumerate(pieces)]
    slope_in = pltpu.make_async_copy(s1h, s1, lsem.at[0])
    weight_in = pltpu.make_async_copy(w1h, w1, wsem.at[0, 0])
    for copy in [first_in] + v_in:
        copy.start()
    small.ready()
    first_in.wait()
    for i, n in enumerate(pieces):
        v_in[i].wait()
        if i == 1:
            slope_in.start()
            weight_in.start()
            low_in.start()
        part = mm_cols(dp2[...].reshape(steps * rows, units), v2[n, :])
        dz[:, :, n] = part.reshape(steps, rows, n.size)

    def out_copy(t):
        return pltpu.make_async_copy(dp1.at[t], dp1h.at[t], osem.at[t])

    slope_in.wait()
    weight_in.wait()
    back_steps(steps, dh, (bufa, bufb), dp1, w1, lambda n: rates[0:1, n], dz, s1, None, None)
    low_in.wait()
    if partners:
        me = lax.axis_index("wide")
        cols = [me] + [jnp.bitwise_xor(me, k) for k in partners]
        half = units // 2
        outs = (send_a.at[pl.ds(0, half)], send_b)
        started = partial_grads(lo1, 1, dp1, cols, width, right, send_ws, gsem, outs)
        own_cols[...] = dp1[:, :, pl.ds(pl.multiple_of(me * width, LANES), width)]
        small.flush(own_cols)
        every = packs[...].reshape(steps * rows, LANES)
        for place in range(2):
            at = pl.ds(pl.multiple_of(cols[place] * width, LANES), width)
            part = mm_rows(every, dp1[:, :, at].reshape(steps * rows, width))
            if place == 0:
                own_v[...] = part
                small.flush(own_v)
            else:
                v_stage[...] = part.astype(BF16)
        started.append(pltpu.make_async_copy(v_stage, send_a.at[pl.ds(half, LANES)], wsem.at[1, 2]))
        started[-1].start()
    else:
        started = [out_copy(t) for t in range(steps)]
        for copy in started:
            copy.start()
    at = pl.ds(pl.multiple_of(own_rank(members) * shard, shard), shard)
    part = mm_cols(dp1[:, at, :].reshape(steps * shard, units), wx[...])
    for t in range(steps):
        combined[:, t, :] = readout[:, t, :] + part[t * shard : (t + 1) * shard]
    small.flush(combined)
    for copy in started:
        copy.wait()


def own_kernel(lo1, lo2, dp1, dp2, wa, va, wb, vb, w_two, v_two, w_one):
    steps, rows, width = dp2.shape
    tile = lo1.shape[2]
    side = pl.program_id(0)
    got_w = jnp.where(side == 0, wa[...], wb[...]).astype(F32)
    got_v = jnp.where(side == 0, va[...], vb[...]).astype(F32)

    def product(left, right, shift):
        count = steps - shift
        return mm_rows(left[:count].reshape(count * rows, tile), right[shift:].reshape(count * rows, width))

    w_two[...] = got_w + product(lo2, dp2, 1)
    v_two[...] = got_v + product(lo1, dp2, 0)
    w_one[...] = product(lo1, dp1, 1)


def own_columns(lo1, lo2, dp1, dp2, got_a, got_b):
    steps, rows, units = lo1.shape
    width = dp1.shape[2]
    many = units // 2 // TILE
    low = pl.BlockSpec((steps, rows, TILE), lambda s, m: (0, 0, s * many + m))
    dp = pl.BlockSpec((steps, rows, width), lambda s, m: (0, 0, 0))
    got = [
        pl.BlockSpec((TILE, width), functools.partial(lambda a, b, s, m: (b + jnp.where(s == a, m, 0), 0), a, b))
        for a, b in ((0, 0), (0, many), (1, 0), (1, many))
    ]
    out = pl.BlockSpec((TILE, width), lambda s, m: (s * many + m, 0))
    return pl.pallas_call(
        own_kernel,
        grid=(2, many),
        in_specs=[low, low, dp, dp] + got,
        out_specs=[out] * 3,
        out_shape=[jax.ShapeDtypeStruct((units, width), F32)] * 3,
        cost_estimate=pl.CostEstimate(
            flops=6 * steps * rows * units * width, bytes_accessed=17 << 20, transcendentals=0
        ),
        compiler_params=pltpu.CompilerParams(vmem_limit_bytes=60 << 20),
    )(lo1, lo2, dp1, dp2, got_a, got_a, got_b, got_b)


def tree(parts):
    while len(parts) > 1:
        parts = [x + y for x, y in zip(parts[::2], parts[1::2])]
    return parts[0]


def join_kernel(first, many, *refs):
    own, wa, wb, own_v, va, bias = refs[:6]
    parts, (w_one, v_one, input_grad, output) = refs[6:-4], refs[-4:]
    side, m = pl.program_id(0), pl.program_id(1)
    w_one[0] = own[...] + jnp.where(side == 0, wa[...], wb[...]).astype(F32)

    @pl.when((side == 0) & (m == 0))
    def _():
        v_one[:, 0, :] = (own_v[...] + va[...].astype(F32))[: v_one.shape[0]]
        total = tree([part[...] for part in parts])
        input_grad[...] = total[:, :, : input_grad.shape[2]]
        outputs, piece, shard = output.shape
        which = lax.axis_index("narrow") * piece
        for i in range(piece):
            row = jnp.zeros((shard, LANES), F32)
            for t in range(total.shape[1]):
                row = jnp.where(which + i == t, total[:, t, :], row)
            output[:, i, :] = (row + bias[...]).T[first : first + outputs]


def joined(own_w1, got_a, got_b, own_v1, bias, parts, width_in, outputs):
    units, width = own_w1.shape
    many = units // 2 // TILE
    shard, steps, lanes = parts[0].shape
    piece = steps // len(parts)
    shape = jax.ShapeDtypeStruct

    def fixed(*size):
        return pl.BlockSpec(size, lambda s, m: (0,) * len(size))

    w_one, v_one, input_grad, output = pl.pallas_call(
        functools.partial(join_kernel, width_in, many),
        grid=(2, many),
        in_specs=[
            pl.BlockSpec((TILE, width), lambda s, m: (s * many + m, 0)),
            pl.BlockSpec((TILE, width), lambda s, m: (jnp.where(s == 0, m, many - 1), 0)),
            pl.BlockSpec((TILE, width), lambda s, m: (jnp.where(s == 1, m, 0), 0)),
            fixed(LANES, width),
            pl.BlockSpec((LANES, width), lambda s, m: (units // 2 // LANES, 0)),
            fixed(1, LANES),
        ]
        + [fixed(shard, steps, lanes)] * len(parts),
        out_specs=[
            pl.BlockSpec((1, TILE, width), lambda s, m: (0, s * many + m, 0)),
            fixed(width_in, 1, width),
            fixed(shard, steps, width_in),
            fixed(outputs, piece, shard),
        ],
        out_shape=[
            shape((1, units, width), F32),
            shape((width_in, 1, width), F32),
            shape((shard, steps, width_in), F32),
            shape((outputs, piece, shard), F32),
        ],
        cost_estimate=pl.CostEstimate(flops=1 << 20, bytes_accessed=6 << 20, transcendentals=0),
        compiler_params=pltpu.CompilerParams(vmem_limit_bytes=JOIN << 20),
    )(own_w1, got_a, got_b, own_v1, got_a, bias, *parts)
    return w_one, jnp.transpose(v_one, (1, 0, 2)), input_grad, jnp.transpose(output, (2, 1, 0))


class Small:
    def __init__(self, loads, stores):
        self.loads, self.stores, self.flying = loads, stores, []

    def ready(self):
        for copy in self.loads:
            copy.wait()

    def flush(self, ref):
        for held, copy in self.stores:
            if held is ref:
                copy.start()
                self.flying.append(copy)


def call(kernel, outs, out_specs, in_specs, scratch, flops, moved, mib):
    def build(*args):
        ins = [i for i, spec in enumerate(in_specs) if spec is VMEM]
        res = [i for i, spec in enumerate(out_specs) if spec is VMEM]
        held = [pltpu.VMEM(args[i].shape, args[i].dtype) for i in ins]
        held += [pltpu.VMEM(outs[i].shape, outs[i].dtype) for i in res]

        def wrapped(*refs):
            refs, sems = list(refs[:-1]), refs[-1]
            rest, here = refs[: len(refs) - len(held)], refs[len(refs) - len(held) :]
            loads, stores = [], []
            for k, i in enumerate(ins):
                loads.append(pltpu.make_async_copy(rest[i], here[k], sems.at[k]))
                rest[i] = here[k]
            for k, i in enumerate(res, len(ins)):
                stores.append((here[k], pltpu.make_async_copy(here[k], rest[len(args) + i], sems.at[k])))
                rest[len(args) + i] = here[k]
            for copy in loads:
                copy.start()
            small = Small(loads, stores)
            kernel(small, *rest)
            for copy in small.flying:
                copy.wait()

        return pl.pallas_call(
            wrapped,
            out_shape=outs,
            in_specs=[ANY] * len(in_specs),
            out_specs=[ANY] * len(outs),
            scratch_shapes=scratch + held + [pltpu.SemaphoreType.DMA((max(len(held), 1),))],
            cost_estimate=pl.CostEstimate(flops=flops, bytes_accessed=moved, transcendentals=0),
            compiler_params=pltpu.CompilerParams(vmem_limit_bytes=mib << 20),
        )(*args)

    return build


def on_device(
    inputs, cotangent, step_mask, washout, lengths, leak_groups, leak_two, w_one, v_one, v_two, w_two, w_out, b_out
):
    shard, steps, width_in = inputs.shape
    outputs = cotangent.shape[2]
    units = w_one.shape[1]
    wide, narrow = lax.axis_size("wide"), lax.axis_size("narrow")
    sets = max(wide // 4, 1)
    members = [d for d in range(wide) if set_of(d, sets) == 0]
    rows = shard * len(members)
    lanes = width_in + outputs + 1
    width = units // wide
    paired = sets == 2 and width % LANES == 0
    partners = (1, 2) if paired else ()
    shape = jax.ShapeDtypeStruct

    def across(x, axis, k):
        size = lax.axis_size(axis)
        return lax.ppermute(x, axis, [(i, i ^ k) for i in range(size)])

    position = jnp.arange(steps, dtype=jnp.int32)[None, :]
    valid = (step_mask == 1) & (position >= washout[:, None]) & (position < lengths[:, None])
    dy = jnp.where(valid[:, :, None], cotangent, jnp.zeros_like(cotangent))
    pack = jnp.concatenate(
        [inputs, dy, valid[:, :, None].astype(BF16), jnp.zeros((shard, steps, LANES - lanes), BF16)], axis=2
    )
    blocks = [pack] + [across(pack, "wide", d) for d in members[1:]]

    wx = jnp.pad(v_one[0], ((0, LANES - width_in), (0, 0)))
    wg = jnp.pad(w_out.T, ((width_in, LANES - width_in - outputs), (0, 0)))
    bias = jnp.pad(b_out[None], ((0, 0), (width_in, LANES - width_in - outputs)))
    rates = jnp.where(leak_groups[:, 0] == 0, F32(0.3), leak_two[0])

    unit = 2 * units * units
    low_t = shape((steps, rows, units), BF16)
    slope_t = shape((steps, rows, units), SLOPE)
    weight_s = pltpu.VMEM((units, units), BF16)
    low_s = pltpu.VMEM((steps, rows, units), BF16)
    full_s = pltpu.VMEM((steps, rows, units), F32)
    slope_s = pltpu.VMEM((steps, rows, units), SLOPE)
    row_s = pltpu.VMEM((rows, units), BF16)
    state_s = pltpu.VMEM((rows, units), F32)
    dma = pltpu.SemaphoreType.DMA

    weight_t = shape((units, units), BF16)
    lo1, lo2, s1, s2, w1t, w2t, stats, packs = call(
        functools.partial(forward_kernel, members, lanes),
        [low_t] * 2 + [slope_t] * 2 + [weight_t] * 2 + [shape((16, units + LANES), F32), shape((steps, rows, LANES), BF16)],
        [ANY] * 6 + [VMEM] * 2,
        [VMEM] * (len(members) + 2) + [ANY] * 3,
        [weight_s] * 3 + [low_s] * 2 + [slope_s] * 2 + [row_s] * 2 + [state_s]
        + [pltpu.VMEM((8, units), F32), pltpu.VMEM((2, 2, units, units // steps), BF16)]
        + [pltpu.VMEM((shard, steps, LANES), F32)]
        + [dma((3, units // TILE)), dma((2, steps)), dma((2, 2))],
        23 * rows * unit, 48 << 20, 60,
    )(*blocks, wx, rates, w_one[0], v_two[0], w_two[0])

    k = 1
    while k * 2 < sets:
        stats = stats + across(stats, "wide", k)
        k *= 2
    other = across(stats, "wide", k) if sets > 1 else jnp.zeros_like(stats)

    cols_t = shape((steps, rows, width), BF16)
    right_s = pltpu.VMEM((2, steps * rows, width), BF16)
    grads_s = pltpu.VMEM((units, width), BF16)
    chunk_n = units // TILE
    result = call(
        functools.partial(back_two_kernel, members, lanes, partners, width),
        [shape((shard, steps, LANES), F32), shape((outputs, units), F32), shape((1, outputs), F32), low_t]
        + ([cols_t] + [shape((units, width), BF16)] * 2 if paired else []),
        [VMEM] * 3 + [ANY] + ([VMEM, ANY, ANY] if paired else []),
        [VMEM] * 5 + [ANY] * 4,
        [low_s] * 2 + [slope_s, weight_s, low_s, low_s, state_s, row_s, row_s, pltpu.VMEM((8, units), F32)]
        + [pltpu.VMEM((steps * shard, units), BF16), dma((6 + units // TILE,))]
        + ([right_s, grads_s, grads_s, dma((2, 2))] if paired else []),
        8 * rows * unit, 40 << 20, 60,
    )(stats, other, wg, rates, packs, lo1, lo2, s2, w2t)
    readout, gwo, gbo, dp2 = result[:4]

    result_one = call(
        functools.partial(back_one_kernel, members, partners, width),
        [shape((shard, steps, LANES), F32), low_t]
        + ([cols_t, shape((LANES, width), F32)] if paired else [])
        + ([shape((units // 2 + LANES, width), BF16), shape((units // 2, width), BF16)] if paired else []),
        [VMEM, ANY] + ([VMEM, VMEM, ANY, ANY] if paired else []),
        [VMEM] * 4 + [ANY] * 5,
        [low_s, weight_s, full_s, weight_s, slope_s, low_s, low_s, state_s, row_s, row_s]
        + [dma((8,)), dma((steps,)), dma((2, chunk_n)), dma((steps,))]
        + ([right_s, grads_s, pltpu.VMEM((LANES, width), BF16), dma((2,))] if paired else []),
        18 * rows * unit, 50 << 20, 60,
    )(wx, rates, packs, readout, dp2, v_two[0], w1t, s1, lo1)
    combined, dp1 = result_one[:2]

    grad_w_out = gwo.T
    grad_b_out = gbo[0]

    parts = [combined] + [across(combined, "narrow", k) for k in range(1, narrow)]
    if paired:
        half = units // 2
        cols_two, send_a, send_b = result[4:]
        got_a, got_b = across(send_a, "wide", 1), across(send_b, "wide", 2)
        cols_one, own_v1, send_a, send_b = result_one[2:]
        got_a, got_b, send_a, send_b = lax.optimization_barrier((got_a, got_b, send_a, send_b))
        grad_w_two, grad_v_two, own_w1 = own_columns(lo1, lo2, cols_one, cols_two, got_a, got_b)
        got_a, got_b = across(send_a, "wide", 1), across(send_b, "wide", 2)
        grad_w_one, grad_v_one, input_grad, output = joined(
            own_w1, got_a, got_b, own_v1, bias, parts, width_in, outputs
        )
    else:
        me = lax.axis_index("wide")
        rank = functools.reduce(lambda a, b: a + b, [((me ^ d) < me).astype(jnp.int32) for d in members[1:]])

        def own_rows(x):
            return lax.dynamic_slice_in_dim(x, rank * shard, shard, 1)

        def summed(left, right):
            part = jnp.einsum("tbr,tbq->rq", left, right, preferred_element_type=F32)
            return lax.psum_scatter(part, "wide", scatter_dimension=1, tiled=True)

        d1, d2, l1, l2, own = (own_rows(x) for x in (dp1, dp2, lo1, lo2, packs))
        grad_w_two = summed(l2[:-1], d2[1:])
        grad_v_two = summed(l1, d2)
        grad_w_one = summed(l1[:-1], d1[1:])
        grad_v_one = summed(own, d1)[:width_in][None]
        grad_w_one = grad_w_one[None]
        total = tree(parts)
        input_grad = total[:, :, :width_in]
        piece = steps // narrow
        mine = lax.dynamic_slice_in_dim(total, lax.axis_index("narrow") * piece, piece, 1)
        output = mine[:, :, width_in : width_in + outputs] + b_out
    return (
        output,
        input_grad,
        grad_w_one,
        grad_v_one,
        grad_v_two[None],
        grad_w_two[None],
        grad_w_out,
        grad_b_out,
    )


def solution(mesh):
    in_specs = (
        P("wide", None, None),
        P("wide", None, None),
        P("wide", None),
        P("wide"),
        P("wide"),
        P(None, "narrow", None),
        P("narrow"),
        P("narrow", None, None),
        P("narrow", None, None),
        P("narrow", None, None),
        P("narrow", None, None),
        P("narrow", None),
        P(),
    )
    out_specs = (
        P("wide", "narrow", None),
        P("wide", None, None),
        P("narrow", None, "wide"),
        P("narrow", None, "wide"),
        P("narrow", None, "wide"),
        P("narrow", None, "wide"),
        P("narrow", None),
        P(),
    )
    return jax.shard_map(on_device, mesh=mesh, in_specs=in_specs, out_specs=out_specs, check_vma=False)
```

```python
import functools

import jax
import jax.numpy as jnp
from jax import lax
from jax.experimental import pallas as pl
from jax.experimental.pallas import tpu as pltpu
from jax.sharding import PartitionSpec as P

F32 = jnp.float32
BF16 = jnp.bfloat16
SLOPE = F32
JOIN = 24
LANES = 128
ROW0 = 96
TILE = 512
VMEM = pl.BlockSpec(memory_space=pltpu.VMEM)
ANY = pl.BlockSpec(memory_space=pl.ANY)
HERE = pl.BlockSpec(memory_space=pltpu.VMEM)
ROWS_T = (((0,), (0,)), ((), ()))
COLS_T = (((1,), (1,)), ((), ()))


def mm(a, b):
    return jnp.dot(a, b, preferred_element_type=F32)


def mm_rows(a, b):
    return lax.dot_general(a, b, ROWS_T, preferred_element_type=F32)


def mm_cols(a, b):
    return lax.dot_general(a, b, COLS_T, preferred_element_type=F32)


def set_of(index, sets):
    return (index ^ (index >> 1)) & (sets - 1)


def tiles(width, tile=TILE):
    return [pl.ds(n, tile) for n in range(0, width, tile)]


def own_rank(members):
    me = lax.axis_index("wide")
    return functools.reduce(
        lambda a, b: a + b, [(jnp.bitwise_xor(me, d) < me).astype(jnp.int32) for d in members[1:]]
    )


def forward_kernel(members, lanes, small, *refs):
    blocks = refs[: len(members)]
    wx, rates, w1h, v2h, w2h = refs[len(members) : len(members) + 5]
    lo1h, lo2h, s1h, s2h, w1th, w2th, stats, packs = refs[len(members) + 5 : len(members) + 13]
    w1 = w1h
    (v2, w2, lo1, lo2, s1, s2, bufa, bufb, h1, ssq, flips, turn, wsem, osem, fsem) = refs[len(members) + 13 :]
    steps, rows, units = lo1.shape
    shard = blocks[0].shape[0]

    small.ready()
    me = lax.axis_index("wide")
    for d, block in zip(members, blocks):
        rank = functools.reduce(
            lambda a, b: a + b,
            [
                (jnp.bitwise_xor(me, e) < jnp.bitwise_xor(me, d)).astype(jnp.int32)
                for e in members
                if e != d
            ],
            jnp.int32(0),
        )
        at = pl.ds(pl.multiple_of(rank * shard, shard), shard)
        turn[...] = block[...].astype(F32)
        for t in range(steps):
            packs[t, at, :] = turn[:, t, :].astype(BF16)
    small.flush(packs)

    def layer_one(t, prev, new, arrive=None):
        for i, n in enumerate(tiles(units)):
            if arrive is not None:
                arrive[i].wait()
            acc = mm(packs[t], wx[:, n])
            if prev is not None:
                acc = acc + mm(prev[...], w1[:, n])
            th = jnp.tanh(acc)
            r = rates[0:1, n]
            if prev is None:
                h = r * th
            else:
                h = h1[:, n]
                h = h + r * (th - h)
            low = h.astype(BF16)
            h1[:, n] = h
            new[:, n] = low
            lo1[t, :, n] = low
            s1[t, :, n] = (r * (1.0 - th * th)).astype(s1.dtype)

    part = units // steps

    def flip_copies(t, slot):
        at = pl.ds(pl.multiple_of(t * part, part), part)
        return [
            pltpu.make_async_copy(flips.at[slot, i], out.at[:, at], fsem.at[slot, i])
            for i, out in enumerate((w1th, w2th))
        ]

    def layer_two(t, prev, new, slot):
        at = pl.ds(pl.multiple_of(t * part, part), part)
        for n in tiles(units):
            acc = mm(lo1[t], v2[:, n])
            if prev is not None:
                acc = acc + mm(prev[...], w2[:, n])
            flips[slot, 0, n, :] = w1[at, n].T
            flips[slot, 1, n, :] = w2[at, n].T
            th = jnp.tanh(acc)
            r = rates[1:2, n]
            if prev is None:
                h = r * th
            else:
                h = h1[:, n]
                h = h + r * (th - h)
            low = h.astype(BF16)
            h1[:, n] = h
            new[:, n] = low
            lo2[t, :, n] = low
            s2[t, :, n] = (r * (1.0 - th * th)).astype(s2.dtype)

    def out_copies(t):
        return [
            pltpu.make_async_copy(src.at[t], dst.at[t], osem.at[i, t])
            for i, (src, dst) in enumerate(((lo2, lo2h), (s2, s2h)))
        ]

    v2_in = pltpu.make_async_copy(v2h, v2, wsem.at[1, 0])
    w2_in = pltpu.make_async_copy(w2h, w2, wsem.at[2, 0])
    lo1_out = pltpu.make_async_copy(lo1, lo1h, wsem.at[1, 1])
    s1_out = pltpu.make_async_copy(s1, s1h, wsem.at[2, 1])

    def pair_one(i, carry):
        t = 2 + 2 * i
        layer_one(t, bufb, bufa)
        layer_one(t + 1, bufa, bufb)
        return carry

    layer_one(0, None, bufa)
    layer_one(1, bufa, bufb)
    v2_in.start()
    w2_in.start()
    lax.fori_loop(0, (steps - 2) // 2, pair_one, 0)
    lo1_out.start()
    s1_out.start()

    def step_two(t, prev, new, slot, reuse):
        if reuse:
            for copy in flip_copies(t - 2, slot):
                copy.wait()
        layer_two(t, prev, new, slot)
        for copy in flip_copies(t, slot) + out_copies(t):
            copy.start()

    def pair_two(i, carry):
        t = 2 + 2 * i
        step_two(t, bufb, bufa, 0, True)
        step_two(t + 1, bufa, bufb, 1, True)
        return carry

    v2_in.wait()
    w2_in.wait()
    step_two(0, None, bufa, 0, False)
    step_two(1, bufa, bufb, 1, False)
    lax.fori_loop(0, (steps - 2) // 2, pair_two, 0)
    every = packs[...].reshape(steps * rows, LANES)
    for t in range(steps):
        valid = jnp.broadcast_to(packs[t][:, lanes - 1 : lanes].astype(F32), (rows, LANES))
        for n in tiles(units, LANES):
            f = lo2[t, :, n].astype(F32)
            squares = jnp.sum((f * f * valid).reshape(rows // 8, 8, LANES), axis=0)
            ssq[:, n] = squares if t == 0 else ssq[:, n] + squares
    for n in tiles(units):
        both = mm_rows(every, lo2[:, :, n].reshape(steps * rows, TILE))
        stats[:, n] = both[ROW0 : ROW0 + 16]
        stats[15:16, n] = jnp.sum(ssq[:, n], axis=0, keepdims=True)
    stats[:, units : units + LANES] = mm_rows(every, every)[ROW0 : ROW0 + 16]
    small.flush(stats)
    lo1_out.wait()
    s1_out.wait()
    for t in range(steps):
        for copy in out_copies(t):
            copy.wait()
    for slot in range(2):
        for copy in flip_copies(steps - 2 + slot, slot):
            copy.wait()


def back_steps(steps, dh, bufs, dp_all, weight, rate_of, extra, slope, weight_in, slope_in):
    units = dh.shape[1]

    def one(t, now, later, arrive=None):
        for i, n in enumerate(tiles(units)):
            if arrive is not None:
                arrive[i].wait()
            r = rate_of(n)
            grad = (1.0 - r) * dh[:, n] + mm(now[...], weight[:, n])
            grad = grad + extra[t - 1, :, n].astype(F32)
            low = (grad * slope[t - 1, :, n].astype(F32)).astype(BF16)
            dh[:, n] = grad
            later[:, n] = low
            dp_all[t - 1, :, n] = low

    def pair(i, carry):
        t = steps - 2 - 2 * i
        one(t, bufs[1], bufs[0])
        one(t - 1, bufs[0], bufs[1])
        return carry

    for n in tiles(units):
        grad = extra[steps - 1, :, n].astype(F32)
        low = (grad * slope[steps - 1, :, n].astype(F32)).astype(BF16)
        dh[:, n] = grad
        bufs[0][:, n] = low
        dp_all[steps - 1, :, n] = low
    one(steps - 1, bufs[0], bufs[1], weight_in)
    if slope_in is not None:
        slope_in.wait()
    lax.fori_loop(0, (steps - 2) // 2, pair, 0)


def partial_grads(left, shift, dp_all, cols, width, right, stage, sems, outs):
    steps, rows, units = left.shape
    half = units // 2
    count = steps - shift
    started = []
    for side in range(2):
        at = pl.ds(pl.multiple_of(cols[1 + side] * width, LANES), width)
        right[side] = dp_all[:, :, at].reshape(steps * rows, width)
    for side in range(2):
        for m in range(0, half, TILE):
            at = pl.ds(side * half + m, TILE)
            l = left[:count, :, at].reshape(count * rows, TILE)
            stage[at, :] = mm_rows(l, right[side, shift * rows :, :]).astype(BF16)
        at = pl.ds(side * half, half)
        started.append(pltpu.make_async_copy(stage.at[at], outs[side], sems.at[side]))
        started[-1].start()
    return started


def back_two_kernel(members, lanes, partners, width, small, *refs):
    st_own, st_other, wg, rates, packs, lo1h, lo2h, s2h, w2h = refs[:9]
    readout, gwo, gbo, dp2h = refs[9:13]
    rest = refs[13:]
    if partners:
        own_cols, send_a, send_b = rest[:3]
        rest = rest[3:]
    lo2, w2 = lo2h, w2h
    (lo1, s2, dp2, dfeat, dh, bufa, bufb, coef, normed, wsem) = rest[:10]
    if partners:
        right, send_ws, send_vs, gsem = rest[10:]
    steps, rows, units = lo2.shape
    shard = rows // len(members)
    last = pl.ds(steps - 2, 2)
    rest_of = pl.ds(0, steps - 2)
    s2_last = pltpu.make_async_copy(s2h.at[last], s2.at[last], wsem.at[1])
    s2_in = pltpu.make_async_copy(s2h.at[rest_of], s2.at[rest_of], wsem.at[5])
    lo1_in = pltpu.make_async_copy(lo1h, lo1, wsem.at[3])
    dp2_out = pltpu.make_async_copy(dp2, dp2h, wsem.at[4])
    small.ready()
    for copy in (s2_last, s2_in, lo1_in):
        copy.start()

    valid_row = lanes - 1 - ROW0
    for n in tiles(units):
        total = st_own[:, n] + st_other[:, n]
        tail = st_own[:, units : units + LANES] + st_other[:, units : units + LANES]
        sums = tail[:, lanes - 1 : lanes]
        count = sums[valid_row : valid_row + 1]
        mean = total[valid_row : valid_row + 1] / count
        inv = lax.rsqrt(total[15:16] / count - mean * mean + 1e-05)
        head = wg[ROW0 : ROW0 + 16, n].astype(F32)
        sum_g = jnp.sum(head * sums, axis=0, keepdims=True)
        sum_gx = jnp.sum(head * total, axis=0, keepdims=True)
        slope = -0.5 * inv * inv * inv * (sum_gx - mean * sum_g)
        shift = -inv * sum_g - 2.0 * mean * slope
        coef[0:1, n] = mean
        coef[1:2, n] = inv
        coef[2:3, n] = shift / count
        coef[3:4, n] = 2.0 * slope / count
        first = valid_row - gwo.shape[0]
        gwo[:, n] = (inv * (total - mean * sums))[first:valid_row]
        gbo[...] = tail[valid_row : valid_row + 1, lanes - 1 - gbo.shape[1] : lanes - 1]

    small.flush(gwo)
    small.flush(gbo)

    def feature_grads(t, carry):
        packed = packs[t]
        valid = packed[:, lanes - 1 : lanes].astype(F32)
        for n in tiles(units):
            grads = mm(packed, wg[:, n])
            values = lo2[t, :, n].astype(F32)
            result = coef[1:2, n] * grads + valid * (coef[2:3, n] + values * coef[3:4, n])
            dfeat[t, :, n] = result.astype(BF16)
        return carry

    lax.fori_loop(0, steps, feature_grads, 0)
    s2_last.wait()
    back_steps(steps, dh, (bufa, bufb), dp2, w2, lambda n: rates[1:2, n], dfeat, s2, None, s2_in)
    dp2_out.start()
    lo1_in.wait()
    started = []
    if partners:
        me = lax.axis_index("wide")
        cols = [me] + [jnp.bitwise_xor(me, k) for k in partners]
        half = pl.ds(0, units // 2)
        outs = (send_a.at[half], send_b.at[half])
        started += partial_grads(lo2, 1, dp2, cols, width, right, send_ws, gsem.at[0], outs)
        half = pl.ds(units // 2, units // 2)
        outs = (send_a.at[half], send_b.at[half])
        started += partial_grads(lo1, 0, dp2, cols, width, right, send_vs, gsem.at[1], outs)
        own_cols[...] = dp2[:, :, pl.ds(pl.multiple_of(me * width, LANES), width)]
        small.flush(own_cols)

    at = pl.ds(pl.multiple_of(own_rank(members) * shard, shard), shard)
    for n in tiles(units):
        values = lo2[:, at, n].astype(F32).reshape(steps * shard, TILE)
        normed[:, n] = ((values - coef[0:1, n]) * coef[1:2, n]).astype(BF16)
    part = mm_cols(normed[...], wg[...])
    for t in range(steps):
        readout[:, t, :] = part[t * shard : (t + 1) * shard]
    small.flush(readout)
    dp2_out.wait()
    for copy in started:
        copy.wait()


def back_one_kernel(members, partners, width, small, *refs):
    wx, rates, packs, readout, dp2h, v2h, w1h, s1h, lo1h = refs[:9]
    combined, dp1h = refs[9:11]
    rest = refs[11:]
    if partners:
        own_cols, own_v, send_a, send_b = rest[:4]
        rest = rest[4:]
    (dp2, v2, dz, w1, s1, lo1, dp1, dh, bufa, bufb, vsem, lsem, wsem, osem) = rest[:14]
    if partners:
        right, send_ws, v_stage, gsem = rest[14:]
    steps, rows, units = dz.shape
    shard = rows // len(members)
    pieces = [pl.ds(0, units // 4), pl.ds(units // 4, units // 4), pl.ds(units // 2, units // 2)]
    first_in = pltpu.make_async_copy(dp2h, dp2, wsem.at[1, 0])
    low_in = pltpu.make_async_copy(lo1h, lo1, wsem.at[1, 1])
    v_in = [pltpu.make_async_copy(v2h.at[n], v2.at[n], vsem.at[i]) for i, n in enumerate(pieces)]
    slope_in = pltpu.make_async_copy(s1h, s1, lsem.at[0])
    weight_in = pltpu.make_async_copy(w1h, w1, wsem.at[0, 0])
    for copy in [first_in] + v_in:
        copy.start()
    small.ready()
    first_in.wait()
    for i, n in enumerate(pieces):
        v_in[i].wait()
        if i == 1:
            slope_in.start()
            weight_in.start()
            low_in.start()
        part = mm_cols(dp2[...].reshape(steps * rows, units), v2[n, :])
        dz[:, :, n] = part.reshape(steps, rows, n.size)

    def out_copy(t):
        return pltpu.make_async_copy(dp1.at[t], dp1h.at[t], osem.at[t])

    slope_in.wait()
    weight_in.wait()
    back_steps(steps, dh, (bufa, bufb), dp1, w1, lambda n: rates[0:1, n], dz, s1, None, None)
    low_in.wait()
    if partners:
        me = lax.axis_index("wide")
        cols = [me] + [jnp.bitwise_xor(me, k) for k in partners]
        half = units // 2
        outs = (send_a.at[pl.ds(0, half)], send_b)
        started = partial_grads(lo1, 1, dp1, cols, width, right, send_ws, gsem, outs)
        own_cols[...] = dp1[:, :, pl.ds(pl.multiple_of(me * width, LANES), width)]
        small.flush(own_cols)
        every = packs[...].reshape(steps * rows, LANES)
        for place in range(2):
            at = pl.ds(pl.multiple_of(cols[place] * width, LANES), width)
            part = mm_rows(every, dp1[:, :, at].reshape(steps * rows, width))
            if place == 0:
                own_v[...] = part
                small.flush(own_v)
            else:
                v_stage[...] = part.astype(BF16)
        started.append(pltpu.make_async_copy(v_stage, send_a.at[pl.ds(half, LANES)], wsem.at[1, 2]))
        started[-1].start()
    else:
        started = [out_copy(t) for t in range(steps)]
        for copy in started:
            copy.start()
    at = pl.ds(pl.multiple_of(own_rank(members) * shard, shard), shard)
    part = mm_cols(dp1[:, at, :].reshape(steps * shard, units), wx[...])
    for t in range(steps):
        combined[:, t, :] = readout[:, t, :] + part[t * shard : (t + 1) * shard]
    small.flush(combined)
    for copy in started:
        copy.wait()


def own_kernel(lo1, lo2, dp1, dp2, wa, va, wb, vb, w_two, v_two, w_one):
    steps, rows, width = dp2.shape
    tile = lo1.shape[2]
    side = pl.program_id(0)
    got_w = jnp.where(side == 0, wa[...], wb[...]).astype(F32)
    got_v = jnp.where(side == 0, va[...], vb[...]).astype(F32)

    def product(left, right, shift):
        count = steps - shift
        return mm_rows(left[:count].reshape(count * rows, tile), right[shift:].reshape(count * rows, width))

    w_two[...] = got_w + product(lo2, dp2, 1)
    v_two[...] = got_v + product(lo1, dp2, 0)
    w_one[...] = product(lo1, dp1, 1)


def own_columns(lo1, lo2, dp1, dp2, got_a, got_b):
    steps, rows, units = lo1.shape
    width = dp1.shape[2]
    tile = units // 2
    many = units // 2 // tile
    low = pl.BlockSpec((steps, rows, tile), lambda s, m: (0, 0, s * many + m))
    dp = pl.BlockSpec((steps, rows, width), lambda s, m: (0, 0, 0))
    got = [
        pl.BlockSpec((tile, width), functools.partial(lambda a, b, s, m: (b + jnp.where(s == a, m, 0), 0), a, b))
        for a, b in ((0, 0), (0, many), (1, 0), (1, many))
    ]
    out = pl.BlockSpec((tile, width), lambda s, m: (s * many + m, 0))
    return pl.pallas_call(
        own_kernel,
        grid=(2, many),
        in_specs=[low, low, dp, dp] + got,
        out_specs=[out] * 3,
        out_shape=[jax.ShapeDtypeStruct((units, width), F32)] * 3,
        cost_estimate=pl.CostEstimate(
            flops=6 * steps * rows * units * width, bytes_accessed=17 << 20, transcendentals=0
        ),
        compiler_params=pltpu.CompilerParams(vmem_limit_bytes=60 << 20),
    )(lo1, lo2, dp1, dp2, got_a, got_a, got_b, got_b)


def tree(parts):
    while len(parts) > 1:
        parts = [x + y for x, y in zip(parts[::2], parts[1::2])]
    return parts[0]


def join_kernel(first, many, *refs):
    own, wa, wb, own_v, va, bias = refs[:6]
    parts, (w_one, v_one, input_grad, output) = refs[6:-4], refs[-4:]
    side, m = pl.program_id(0), pl.program_id(1)
    w_one[0] = own[...] + jnp.where(side == 0, wa[...], wb[...]).astype(F32)

    @pl.when((side == 0) & (m == 0))
    def _():
        v_one[:, 0, :] = (own_v[...] + va[...].astype(F32))[: v_one.shape[0]]
        total = tree([part[...] for part in parts])
        input_grad[...] = total[:, :, : input_grad.shape[2]]
        outputs, piece, shard = output.shape
        which = lax.axis_index("narrow") * piece
        for i in range(piece):
            row = jnp.zeros((shard, LANES), F32)
            for t in range(total.shape[1]):
                row = jnp.where(which + i == t, total[:, t, :], row)
            output[:, i, :] = (row + bias[...]).T[first : first + outputs]


def joined(own_w1, got_a, got_b, own_v1, bias, parts, width_in, outputs):
    units, width = own_w1.shape
    many = units // 2 // TILE
    shard, steps, lanes = parts[0].shape
    piece = steps // len(parts)
    shape = jax.ShapeDtypeStruct

    def fixed(*size):
        return pl.BlockSpec(size, lambda s, m: (0,) * len(size))

    w_one, v_one, input_grad, output = pl.pallas_call(
        functools.partial(join_kernel, width_in, many),
        grid=(2, many),
        in_specs=[
            pl.BlockSpec((TILE, width), lambda s, m: (s * many + m, 0)),
            pl.BlockSpec((TILE, width), lambda s, m: (jnp.where(s == 0, m, many - 1), 0)),
            pl.BlockSpec((TILE, width), lambda s, m: (jnp.where(s == 1, m, 0), 0)),
            fixed(LANES, width),
            pl.BlockSpec((LANES, width), lambda s, m: (units // 2 // LANES, 0)),
            fixed(1, LANES),
        ]
        + [fixed(shard, steps, lanes)] * len(parts),
        out_specs=[
            pl.BlockSpec((1, TILE, width), lambda s, m: (0, s * many + m, 0)),
            fixed(width_in, 1, width),
            fixed(shard, steps, width_in),
            fixed(outputs, piece, shard),
        ],
        out_shape=[
            shape((1, units, width), F32),
            shape((width_in, 1, width), F32),
            shape((shard, steps, width_in), F32),
            shape((outputs, piece, shard), F32),
        ],
        cost_estimate=pl.CostEstimate(flops=1 << 20, bytes_accessed=6 << 20, transcendentals=0),
        compiler_params=pltpu.CompilerParams(vmem_limit_bytes=JOIN << 20),
    )(own_w1, got_a, got_b, own_v1, got_a, bias, *parts)
    return w_one, jnp.transpose(v_one, (1, 0, 2)), input_grad, jnp.transpose(output, (2, 1, 0))


class Small:
    def __init__(self, loads, stores):
        self.loads, self.stores, self.flying = loads, stores, []

    def ready(self):
        for copy in self.loads:
            copy.wait()

    def flush(self, ref):
        for held, copy in self.stores:
            if held is ref:
                copy.start()
                self.flying.append(copy)


def call(kernel, outs, out_specs, in_specs, scratch, flops, moved, mib):
    def build(*args):
        ins = [i for i, spec in enumerate(in_specs) if spec is VMEM]
        res = [i for i, spec in enumerate(out_specs) if spec is VMEM]
        held = [pltpu.VMEM(args[i].shape, args[i].dtype) for i in ins]
        held += [pltpu.VMEM(outs[i].shape, outs[i].dtype) for i in res]

        def wrapped(*refs):
            refs, sems = list(refs[:-1]), refs[-1]
            rest, here = refs[: len(refs) - len(held)], refs[len(refs) - len(held) :]
            loads, stores = [], []
            for k, i in enumerate(ins):
                loads.append(pltpu.make_async_copy(rest[i], here[k], sems.at[k]))
                rest[i] = here[k]
            for k, i in enumerate(res, len(ins)):
                stores.append((here[k], pltpu.make_async_copy(here[k], rest[len(args) + i], sems.at[k])))
                rest[len(args) + i] = here[k]
            for copy in loads:
                copy.start()
            small = Small(loads, stores)
            kernel(small, *rest)
            for copy in small.flying:
                copy.wait()

        return pl.pallas_call(
            wrapped,
            out_shape=outs,
            in_specs=[HERE if spec is HERE else ANY for spec in in_specs],
            out_specs=[ANY] * len(outs),
            scratch_shapes=scratch + held + [pltpu.SemaphoreType.DMA((max(len(held), 1),))],
            cost_estimate=pl.CostEstimate(flops=flops, bytes_accessed=moved, transcendentals=0),
            compiler_params=pltpu.CompilerParams(vmem_limit_bytes=mib << 20),
        )(*args)

    return build


def preload_kernel(*refs):
    half = len(refs) // 2
    sems = refs[-1]
    copies = [pltpu.make_async_copy(refs[i], refs[half + i], sems.at[i]) for i in range(half)]
    for copy in copies:
        copy.start()
    for copy in copies:
        copy.wait()


def preloaded(*arrays):
    size = sum(a.size * a.dtype.itemsize for a in arrays)
    return pl.pallas_call(
        preload_kernel,
        in_specs=[ANY] * len(arrays),
        out_specs=[HERE] * len(arrays),
        out_shape=[pltpu.VMEM(a.shape, a.dtype) for a in arrays],
        scratch_shapes=[pltpu.SemaphoreType.DMA((len(arrays),))],
        cost_estimate=pl.CostEstimate(flops=0, bytes_accessed=size, transcendentals=0),
        compiler_params=pltpu.CompilerParams(vmem_limit_bytes=1 << 20),
    )(*[pltpu.with_memory_space_constraint(a, pltpu.HBM) for a in arrays])


def here(x):
    return pltpu.with_memory_space_constraint(x, pltpu.VMEM)


def on_device(
    inputs, cotangent, step_mask, washout, lengths, leak_groups, leak_two, w_one, v_one, v_two, w_two, w_out, b_out
):
    shard, steps, width_in = inputs.shape
    outputs = cotangent.shape[2]
    units = w_one.shape[1]
    wide, narrow = lax.axis_size("wide"), lax.axis_size("narrow")
    sets = max(wide // 4, 1)
    members = [d for d in range(wide) if set_of(d, sets) == 0]
    rows = shard * len(members)
    lanes = width_in + outputs + 1
    width = units // wide
    paired = sets == 2 and width % LANES == 0
    partners = (1, 2) if paired else ()
    shape = jax.ShapeDtypeStruct

    def across(x, axis, k):
        size = lax.axis_size(axis)
        return lax.ppermute(x, axis, [(i, i ^ k) for i in range(size)])

    position = jnp.arange(steps, dtype=jnp.int32)[None, :]
    valid = (step_mask == 1) & (position >= washout[:, None]) & (position < lengths[:, None])
    dy = jnp.where(valid[:, :, None], cotangent, jnp.zeros_like(cotangent))
    pack = jnp.concatenate(
        [inputs, dy, valid[:, :, None].astype(BF16), jnp.zeros((shard, steps, LANES - lanes), BF16)], axis=2
    )
    blocks = [pack] + [across(pack, "wide", d) for d in members[1:]]

    wx = jnp.pad(v_one[0], ((0, LANES - width_in), (0, 0)))
    wg = jnp.pad(w_out.T, ((width_in, LANES - width_in - outputs), (0, 0)))
    bias = jnp.pad(b_out[None], ((0, 0), (width_in, LANES - width_in - outputs)))
    rates = jnp.where(leak_groups[:, 0] == 0, F32(0.3), leak_two[0])

    unit = 2 * units * units
    low_t = shape((steps, rows, units), BF16)
    slope_t = shape((steps, rows, units), SLOPE)
    weight_s = pltpu.VMEM((units, units), BF16)
    low_s = pltpu.VMEM((steps, rows, units), BF16)
    full_s = pltpu.VMEM((steps, rows, units), F32)
    slope_s = pltpu.VMEM((steps, rows, units), SLOPE)
    row_s = pltpu.VMEM((rows, units), BF16)
    state_s = pltpu.VMEM((rows, units), F32)
    dma = pltpu.SemaphoreType.DMA

    weight_t = shape((units, units), BF16)
    (w1_near,) = preloaded(w_one[0])
    lo1, lo2, s1, s2, w1t, w2t, stats, packs = call(
        functools.partial(forward_kernel, members, lanes),
        [low_t] * 2 + [slope_t] * 2 + [weight_t] * 2 + [shape((16, units + LANES), F32), shape((steps, rows, LANES), BF16)],
        [ANY] * 6 + [VMEM] * 2,
        [HERE] * (len(members) + 3) + [ANY] * 2,
        [weight_s] * 2 + [low_s] * 2 + [slope_s] * 2 + [row_s] * 2 + [state_s]
        + [pltpu.VMEM((8, units), F32), pltpu.VMEM((2, 2, units, units // steps), BF16)]
        + [pltpu.VMEM((shard, steps, LANES), F32)]
        + [dma((3, units // TILE)), dma((2, steps)), dma((2, 2))],
        23 * rows * unit, 48 << 20, 50,
    )(*[here(x) for x in (*blocks, wx, rates)], here(w1_near), v_two[0], w_two[0])

    k = 1
    while k * 2 < sets:
        stats = stats + across(stats, "wide", k)
        k *= 2
    other = across(stats, "wide", k) if sets > 1 else jnp.zeros_like(stats)

    w2t_near, lo2_near = preloaded(w2t, lo2)
    cols_t = shape((steps, rows, width), BF16)
    right_s = pltpu.VMEM((2, steps * rows, width), BF16)
    grads_s = pltpu.VMEM((units, width), BF16)
    chunk_n = units // TILE
    result = call(
        functools.partial(back_two_kernel, members, lanes, partners, width),
        [shape((shard, steps, LANES), F32), shape((outputs, units), F32), shape((1, outputs), F32), low_t]
        + ([cols_t] + [shape((units, width), BF16)] * 2 if paired else []),
        [VMEM] * 3 + [ANY] + ([VMEM, ANY, ANY] if paired else []),
        [VMEM, HERE] + [VMEM] * 3 + [ANY, HERE, ANY, HERE],
        [low_s, slope_s, low_s, low_s, state_s, row_s, row_s, pltpu.VMEM((8, units), F32)]
        + [pltpu.VMEM((steps * shard, units), BF16), dma((6 + units // TILE,))]
        + ([right_s, grads_s, grads_s, dma((2, 2))] if paired else []),
        8 * rows * unit, 40 << 20, 44,
    )(stats, here(other), wg, rates, packs, lo1, here(lo2_near), s2, here(w2t_near))
    readout, gwo, gbo, dp2 = result[:4]

    result_one = call(
        functools.partial(back_one_kernel, members, partners, width),
        [shape((shard, steps, LANES), F32), low_t]
        + ([cols_t, shape((LANES, width), F32)] if paired else [])
        + ([shape((units // 2 + LANES, width), BF16), shape((units // 2, width), BF16)] if paired else []),
        [VMEM, ANY] + ([VMEM, VMEM, ANY, ANY] if paired else []),
        [VMEM] * 4 + [ANY] * 5,
        [low_s, weight_s, full_s, weight_s, slope_s, low_s, low_s, state_s, row_s, row_s]
        + [dma((8,)), dma((steps,)), dma((2, chunk_n)), dma((steps,))]
        + ([right_s, grads_s, pltpu.VMEM((LANES, width), BF16), dma((2,))] if paired else []),
        18 * rows * unit, 50 << 20, 60,
    )(wx, rates, packs, readout, dp2, v_two[0], w1t, s1, lo1)
    combined, dp1 = result_one[:2]

    grad_w_out = gwo.T
    grad_b_out = gbo[0]

    parts = [combined] + [across(combined, "narrow", k) for k in range(1, narrow)]
    if paired:
        half = units // 2
        cols_two, send_a, send_b = result[4:]
        got_a, got_b = across(send_a, "wide", 1), across(send_b, "wide", 2)
        cols_one, own_v1, send_a, send_b = result_one[2:]
        got_a, got_b, send_a, send_b = lax.optimization_barrier((got_a, got_b, send_a, send_b))
        grad_w_two, grad_v_two, own_w1 = own_columns(lo1, lo2, cols_one, cols_two, got_a, got_b)
        got_a, got_b = across(send_a, "wide", 1), across(send_b, "wide", 2)
        grad_w_one, grad_v_one, input_grad, output = joined(
            own_w1, got_a, got_b, own_v1, bias, parts, width_in, outputs
        )
    else:
        me = lax.axis_index("wide")
        rank = functools.reduce(lambda a, b: a + b, [((me ^ d) < me).astype(jnp.int32) for d in members[1:]])

        def own_rows(x):
            return lax.dynamic_slice_in_dim(x, rank * shard, shard, 1)

        def summed(left, right):
            part = jnp.einsum("tbr,tbq->rq", left, right, preferred_element_type=F32)
            return lax.psum_scatter(part, "wide", scatter_dimension=1, tiled=True)

        d1, d2, l1, l2, own = (own_rows(x) for x in (dp1, dp2, lo1, lo2, packs))
        grad_w_two = summed(l2[:-1], d2[1:])
        grad_v_two = summed(l1, d2)
        grad_w_one = summed(l1[:-1], d1[1:])
        grad_v_one = summed(own, d1)[:width_in][None]
        grad_w_one = grad_w_one[None]
        total = tree(parts)
        input_grad = total[:, :, :width_in]
        piece = steps // narrow
        mine = lax.dynamic_slice_in_dim(total, lax.axis_index("narrow") * piece, piece, 1)
        output = mine[:, :, width_in : width_in + outputs] + b_out
    return (
        output,
        input_grad,
        grad_w_one,
        grad_v_one,
        grad_v_two[None],
        grad_w_two[None],
        grad_w_out,
        grad_b_out,
    )


def solution(mesh):
    in_specs = (
        P("wide", None, None),
        P("wide", None, None),
        P("wide", None),
        P("wide"),
        P("wide"),
        P(None, "narrow", None),
        P("narrow"),
        P("narrow", None, None),
        P("narrow", None, None),
        P("narrow", None, None),
        P("narrow", None, None),
        P("narrow", None),
        P(),
    )
    out_specs = (
        P("wide", "narrow", None),
        P("wide", None, None),
        P("narrow", None, "wide"),
        P("narrow", None, "wide"),
        P("narrow", None, "wide"),
        P("narrow", None, "wide"),
        P("narrow", None),
        P(),
    )
    return jax.shard_map(on_device, mesh=mesh, in_specs=in_specs, out_specs=out_specs, check_vma=False)
```
